32 devices in a mesh: patch: 8 (over z, x), tile: 4 (over y, core).
Axes of the slice: x: 2, y: 2, z: 4, core: 2. Of those that a mesh axis runs over, the one named last changes fastest.
Arguments:
- latents: float32 [1088, 128], P('patch')
- timestamps: int32 [1088], P('patch'), may hold values from 0 to 56, as said below
- cell_map: int32 [1024], replicated, may hold values from 0 to 1023, as said below
- w_video: bfloat16 [128, 3072], replicated, may hold values from -0.5 to 0.5
- w_audio: bfloat16 [128, 3072], replicated, may hold values from -0.5 to 0.5
- mod_scale: float32 [2, 3072], replicated, may hold values from -3 to 3
- mod_shift: float32 [2, 3072], replicated, may hold values from -3 to 3
- w_query: bfloat16 [3072, 3072], P(None, 'tile')
- w_key: bfloat16 [3072, 3072], P(None, 'tile')
- w_value: bfloat16 [3072, 3072], P(None, 'tile'), may hold values from -0.109375 to 0.109375
- q_gain: float32 [3072], P('tile'), as said below
- k_gain: float32 [3072], P('tile'), as said below
- k_cache: bfloat16 [1088, 3072], P('patch', 'tile'), may hold values from -8 to 8
- v_cache: bfloat16 [1088, 3072], P('patch', 'tile'), may hold values from -6 to 6
- w_out: bfloat16 [3072, 3072], P('tile'), may hold values from -0.109375 to 0.109375
- out_gain: float32 [3072], replicated, may hold values from 0.25 to 1.75
- w_final: bfloat16 [3072, 128], replicated, may hold values from -0.109375 to 0.109375
- step_sizes: float32 [2], replicated, may hold values from 0.2 to 0.6
- conv_w: bfloat16 [3, 3, 3, 128, 512], replicated, may hold values from -0.109375 to 0.109375
- conv_b: float32 [512], replicated, may hold values from -3 to 3
Outputs:
- final_latents: float32 [1088, 128], P('patch')
- decoded: bfloat16 [8, 16, 8, 512], P(None, 'patch', 'tile')
The draws below stay inside these ranges and needn't reach their ends.
Inputs may be any that keep to these rules, and one draw needn't show every extreme that they name: `cell_map`: a permutation of the 1024 cells of the grid; entry r is the cell of the r-th video token, which stands in patch shard r // 128; cell (f, h, w) belongs to the decode block (h // 2, w // 2), held by patch index h // 2 and tile index w // 2; every patch shard holds exactly 4 cells of every decode block. A video token's timestamp is 8 times the frame of its cell; audio tokens' timestamps lie in the same span. `q_gain`: positive. `k_gain`: positive.
All inputs are finite; a program needn't handle non-finite values.
Results may differ from the reference program's by a relative error of at most 0.009.
Values may be sent and summed in bfloat16 or wider, within the bound.
A program may use at most 128 MiB of HBM per device.

```python
import jax
import jax.numpy as jnp
from jax import lax

HEADS = 24
HEAD = 128
D = 3072
C = 128
CO = 512
VID_DEV = 128
AUD_DEV = 8
TOK_DEV = 136
TOKENS = 1088
STEPS = 2
FRAMES = 8
BH = 2
BW = 2
HH = 16
WW = 8
CELLS = 32
COUNT = 4
VID_TOTAL = 1024
N_PATCH = 8
N_TILE = 4
DEVICES = 32


def permute_cells(single_key):
    return jax.random.permutation(single_key, CELLS)


def permute_tokens(single_key):
    return jax.random.permutation(single_key, VID_DEV)


def cell_layout(key):
    base_key = jax.random.fold_in(key, 7)
    device_key, shard_key = jax.random.split(base_key)
    local_order = jax.vmap(permute_cells)(jax.random.split(device_key, DEVICES))
    device_ids = jnp.arange(DEVICES, dtype=jnp.int32)[:, None]
    owner_row = device_ids // N_TILE
    owner_column = device_ids % N_TILE
    frame_ids = local_order // (BH * BW)
    inner_row = local_order // BW % BH
    inner_column = local_order % BW
    global_cell = (frame_ids * HH + owner_row * BH + inner_row) * WW + owner_column * BW + inner_column
    by_shard = global_cell.reshape(DEVICES, N_PATCH, COUNT).transpose(1, 0, 2).reshape(N_PATCH, VID_DEV)
    shard_order = jax.vmap(permute_tokens)(jax.random.split(shard_key, N_PATCH))
    shuffled = jnp.take_along_axis(by_shard, shard_order, axis=1)
    return shuffled.reshape(-1).astype(jnp.int32)


def draw_cell_map(key, part):
    return cell_layout(key)


def draw_timestamps(key, part):
    cell_list = cell_layout(key)
    video_times = (cell_list // (HH * WW)).reshape(N_PATCH, VID_DEV) * 8
    audio_times = jax.random.randint(jax.random.fold_in(key, 13), (N_PATCH, AUD_DEV), 0, 8 * FRAMES - 7)
    return jnp.concatenate([video_times, audio_times], axis=1).reshape(-1).astype(jnp.int32)


def paired_weights(key):
    left_matrix = jax.random.normal(jax.random.fold_in(key, 41), (D, D), jnp.float32) * D ** (-0.5)
    right_matrix = jax.random.normal(jax.random.fold_in(key, 43), (D, D), jnp.float32) * D ** (-0.5)
    return (left_matrix, right_matrix)


def draw_w_query(key, part):
    return paired_weights(key)[0].astype(jnp.bfloat16)


def draw_w_key(key, part):
    return paired_weights(key)[1].astype(jnp.bfloat16)


def paired_gain(key, salt):
    spread = jnp.exp(jax.random.uniform(jax.random.fold_in(key, salt), (D,), jnp.float32, 0.0, 0.9163))
    return spread


def draw_q_gain(key, part):
    return paired_gain(key, 61)


def draw_k_gain(key, part):
    return paired_gain(key, 67)


def draw_latents(key, part):
    values = jax.random.normal(jax.random.fold_in(key, 51), (TOKENS, C), jnp.float32)
    return jnp.clip(values, -8.0, 8.0)


def shard_levels(rng, shape, cuts, least, top_value):
    level = 1.0
    for dim, blocks in cuts:
        steps = jax.random.uniform(jax.random.fold_in(jax.random.fold_in(rng, 6), dim), (blocks,), jnp.float32, least / len(cuts), top_value / len(cuts))
        level = level * jnp.repeat(jnp.exp(steps), shape[dim] // blocks).reshape((-1,) + (1,) * (len(shape) - 1 - dim))
    return level


def centred(own_key, extent, deviation, most, cuts=(), kind=jnp.bfloat16):
    drawn = deviation * jax.random.normal(own_key, extent, jnp.float32)
    if cuts:
        drawn = drawn * shard_levels(own_key, extent, cuts, -0.22, 0.18)
    return jnp.clip(drawn, -most, most).astype(kind)


def setup_inputs(seed: int = 0) -> dict:
    key_list = jax.random.split(jax.random.key(seed), 21)
    latents = draw_latents(jax.random.fold_in(key_list[20], 71), 0)
    timestamps = draw_timestamps(jax.random.fold_in(key_list[20], 71), 0)
    cell_map = draw_cell_map(jax.random.fold_in(key_list[20], 71), 0)
    w_video = centred(key_list[3], (C, D), C ** -0.5, 0.5)
    w_audio = centred(key_list[4], (C, D), C ** -0.5, 0.5)
    mod_scale = centred(key_list[5], (STEPS, D), 0.5, 3.0, (), jnp.float32)
    mod_shift = centred(key_list[6], (STEPS, D), 0.5, 3.0, (), jnp.float32)
    w_query = draw_w_query(jax.random.fold_in(key_list[20], 71), 0)
    w_key = draw_w_key(jax.random.fold_in(key_list[20], 71), 0)
    w_value = centred(key_list[9], (D, D), D ** -0.5, 0.109375, ((1, 4),))
    q_gain = draw_q_gain(jax.random.fold_in(key_list[20], 71), 0)
    k_gain = draw_k_gain(jax.random.fold_in(key_list[20], 71), 0)
    k_cache = centred(key_list[12], (TOKENS, D), 1.5, 8.0, ((0, 8), (1, 4)))
    v_cache = centred(key_list[13], (TOKENS, D), 1.0, 6.0, ((0, 8), (1, 4)))
    w_out = centred(key_list[14], (D, D), D ** -0.5, 0.109375, ((0, 4),))
    out_gain = jnp.clip(1.0 + 0.15 * jax.random.normal(key_list[15], (D,), jnp.float32), 0.25, 1.75)
    w_final = centred(key_list[16], (D, C), D ** -0.5, 0.109375)
    step_sizes = jnp.clip(jax.random.uniform(key_list[17], (STEPS,), jnp.float32, 0.2, 0.6), 0.2, 0.6)
    conv_w = centred(key_list[18], (3, 3, 3, C, CO), (27 * C) ** -0.5, 0.109375)
    conv_b = centred(key_list[19], (CO,), 0.5, 3.0, (), jnp.float32)
    return dict(latents=latents, timestamps=timestamps, cell_map=cell_map, w_video=w_video, w_audio=w_audio, mod_scale=mod_scale, mod_shift=mod_shift, w_query=w_query, w_key=w_key, w_value=w_value, q_gain=q_gain, k_gain=k_gain, k_cache=k_cache, v_cache=v_cache, w_out=w_out, out_gain=out_gain, w_final=w_final, step_sizes=step_sizes, conv_w=conv_w, conv_b=conv_b)


EPSILON = 1e-06

def row_scaled(matrix):
    return matrix * lax.rsqrt(lax.optimization_barrier(jnp.mean(matrix * matrix, axis=-1, keepdims=True)) + EPSILON)

def rotate(matrix, stamps):
    half_size = matrix.shape[-1] // 2
    frequency = jnp.exp(-jnp.log(10000.0) * jnp.arange(half_size, dtype=jnp.float32) / half_size)
    angles = stamps.astype(jnp.float32)[:, None, None] * frequency
    cosine = jnp.cos(angles)
    sines = jnp.sin(angles)
    leading = matrix[..., :half_size]
    trailing = matrix[..., half_size:]
    return jnp.concatenate([leading * cosine - trailing * sines, leading * sines + trailing * cosine], axis=-1)

def head_project(normed, weight, gain, stamps):
    raw_out = jnp.dot(normed, weight, preferred_element_type=jnp.float32)
    shaped = raw_out.reshape(raw_out.shape[0], HEADS, HEAD)
    scaled = row_scaled(shaped) * gain.reshape(HEADS, HEAD)
    return rotate(scaled, stamps).reshape(raw_out.shape[0], -1).astype(jnp.bfloat16)

def reference(latents, timestamps, cell_map, w_video, w_audio, mod_scale, mod_shift, w_query, w_key, w_value, q_gain, k_gain, k_cache, v_cache, w_out, out_gain, w_final, step_sizes, conv_w, conv_b):
    shard_of = jnp.arange(TOKENS, dtype=jnp.int32) // TOK_DEV
    same_shard = shard_of[:, None] == shard_of[None, :]
    latent_state = latents
    stale_keys = k_cache
    stale_values = v_cache
    scale_factor = HEAD ** (-0.5)
    for step_index in range(STEPS):
        latent_b = latent_state.astype(jnp.bfloat16).reshape(N_PATCH, TOK_DEV, C)
        video_part = jnp.dot(latent_b[:, :VID_DEV].reshape(-1, C), w_video, preferred_element_type=jnp.float32)
        audio_part = jnp.dot(latent_b[:, VID_DEV:].reshape(-1, C), w_audio, preferred_element_type=jnp.float32)
        embedded = jnp.concatenate([video_part.reshape(N_PATCH, VID_DEV, D), audio_part.reshape(N_PATCH, AUD_DEV, D)], axis=1).reshape(TOKENS, D)
        normed = (row_scaled(embedded) * (1.0 + mod_scale[step_index]) + mod_shift[step_index]).astype(jnp.bfloat16)
        queries = head_project(normed, w_query, q_gain, timestamps)
        fresh_keys = head_project(normed, w_key, k_gain, timestamps)
        values = jnp.dot(normed, w_value, preferred_element_type=jnp.float32).astype(jnp.bfloat16)
        old_keys = stale_keys
        old_values = stale_values

        def one_head(head_index):

            def head_slice(matrix):
                return lax.dynamic_slice_in_dim(matrix, head_index * HEAD, HEAD, 1)
            query_head = head_slice(queries)
            fresh_scores = jnp.dot(query_head, head_slice(fresh_keys).T, preferred_element_type=jnp.float32) * scale_factor
            stale_scores = jnp.dot(query_head, head_slice(old_keys).T, preferred_element_type=jnp.float32) * scale_factor
            scores = jnp.where(same_shard, fresh_scores, stale_scores)
            row_top = lax.optimization_barrier(jnp.max(scores, axis=1, keepdims=True))
            weights = jnp.exp(scores - row_top)
            totals = lax.optimization_barrier(jnp.sum(weights, axis=1, keepdims=True))
            rounded = weights.astype(jnp.bfloat16)
            zero_probs = jnp.zeros_like(rounded)
            result = jnp.dot(jnp.where(same_shard, rounded, zero_probs), head_slice(values), preferred_element_type=jnp.float32)
            result = result + jnp.dot(jnp.where(same_shard, zero_probs, rounded), head_slice(old_values), preferred_element_type=jnp.float32)
            return (result / totals).astype(jnp.bfloat16)
        attended = lax.map(one_head, jnp.arange(HEADS, dtype=jnp.int32))
        attended = attended.transpose(1, 0, 2).reshape(TOKENS, D)
        mixed_rows = embedded + jnp.dot(attended, w_out, preferred_element_type=jnp.float32)
        final_normed = (row_scaled(mixed_rows) * out_gain).astype(jnp.bfloat16)
        velocity = jnp.dot(final_normed, w_final, preferred_element_type=jnp.float32)
        latent_state = latent_state - step_sizes[step_index] * velocity
        stale_keys = fresh_keys
        stale_values = values
    video_rows = latent_state.reshape(N_PATCH, TOK_DEV, C)[:, :VID_DEV].reshape(-1, C).astype(jnp.bfloat16)
    latent_grid = jnp.zeros((VID_TOTAL, C), jnp.bfloat16).at[cell_map].set(video_rows).reshape(FRAMES, HH, WW, C)
    padded = jnp.pad(latent_grid, ((1, 1), (1, 1), (1, 1), (0, 0)))
    columns = jnp.concatenate([padded[shift_time:shift_time + FRAMES, shift_row:shift_row + HH, shift_column:shift_column + WW] for shift_time in range(3) for shift_row in range(3) for shift_column in range(3)], axis=-1)
    conv_out = jnp.dot(columns.reshape(VID_TOTAL, 27 * C), conv_w.reshape(27 * C, CO), preferred_element_type=jnp.float32) + conv_b
    decoded = conv_out.astype(jnp.bfloat16).reshape(FRAMES, HH, WW, CO)
    return (latent_state, decoded)
```

```python
import functools

import jax
import jax.numpy as jnp
from jax import lax
from jax.experimental import pallas as pl
from jax.experimental.pallas import tpu as pltpu
from jax.sharding import PartitionSpec as P

HEAD = 128
VID_DEV = 128
AUD_DEV = 8
STEPS = 2
FRAMES = 8
BH = 2
EPSILON = 1e-06
MESH = pl.DeviceIdType.MESH
F32 = jnp.float32
BF16 = jnp.bfloat16


def dot(a, b):
    return jnp.dot(a, b, preferred_element_type=F32)


def kernel(
    n,
    nt,
    latents,
    stamps,
    cells,
    mod_scale,
    mod_shift,
    q_gain,
    k_gain,
    k_cache,
    v_cache,
    out_gain,
    step_sizes,
    conv_b,
    wv_hbm,
    wa_hbm,
    wq_hbm,
    wk_hbm,
    wval_hbm,
    wo_hbm,
    wf_hbm,
    cw_hbm,
    state_out,
    conv_out,
    w_vid,
    w_aud,
    w_qkv,
    w_o,
    w_f,
    w_c,
    kv0,
    kv1,
    lat,
    emb,
    normed,
    embq,
    q_ref,
    cs_ref,
    pair_cs,
    table,
    att,
    o_send,
    p_send,
    p_recv,
    acc,
    s1_send,
    s1_recv,
    s2_send,
    s2_recv,
    vel_send,
    vel_recv,
    vid,
    onehot,
    grown,
    load_sem,
    lz_ss,
    lz_rs,
    lx_ss,
    lx_rs,
    kz_ss,
    kz_rs,
    kx_ss,
    kx_rs,
    o_ss,
    o_rs,
    p_ss,
    p_rs,
    s1_ss,
    s1_rs,
    s2_ss,
    s2_rs,
    v_ss,
    v_rs,
    vid_ss,
    vid_rs,
):
    rows = latents.shape[0]
    pad = kv0.shape[3]
    width = emb.shape[1]
    hw = w_qkv.shape[1] // 3
    nh = hw // HEAD
    quarter = width // nt
    nz = n // 2
    npz = nz // 2
    me = lax.axis_index("patch")
    tile = lax.axis_index("tile")
    core = tile % 2
    ty = tile // 2
    ny = nt // 2
    zz = me // 2
    xx = me % 2
    h = zz % 2
    mate = me + 2 - 4 * h

    def half_cols(a):
        return pl.ds(pl.multiple_of(a * hw, HEAD), hw)

    loads = []
    for i, (src, dst) in enumerate(
        (
            (wv_hbm, w_vid),
            (wa_hbm, w_aud),
            (wk_hbm.at[:, half_cols(h)], w_qkv.at[:, 0:hw]),
            (wval_hbm.at[:, half_cols(h)], w_qkv.at[:, hw : 2 * hw]),
            (wq_hbm.at[:, half_cols(h)], w_qkv.at[:, 2 * hw : 3 * hw]),
            (wo_hbm, w_o),
            (wf_hbm, w_f),
            (cw_hbm, w_c),
        )
    ):
        copy = pltpu.make_async_copy(src, dst, load_sem.at[i])
        copy.start()
        loads.append(copy)

    barrier = pltpu.get_barrier_semaphore()
    for j in range(1, n):
        pl.semaphore_signal(
            barrier, inc=1, device_id=(lax.rem(me + j, n), tile), device_id_type=MESH
        )
    for j in range(1, nt):
        pl.semaphore_signal(
            barrier, inc=1, device_id=(me, lax.rem(tile + j, nt)), device_id_type=MESH
        )

    def padded(x):
        return jnp.concatenate([x, jnp.zeros((pad - rows, x.shape[1]), F32)], axis=0)

    line_row = lax.broadcasted_iota(jnp.int32, (pad - rows, HEAD), 0)
    aud_stamps = jnp.concatenate(
        [stamps[:, VID_DEV:rows], jnp.zeros((1, HEAD - AUD_DEV), jnp.int32)], axis=1
    ).astype(F32)
    vid_stamps = stamps[:, 0:VID_DEV].astype(F32)
    tail = jnp.where(line_row == 0, vid_stamps, jnp.where(line_row == 1, aud_stamps, 0.0))
    lat[xx, zz] = jnp.concatenate([latents[...], tail], axis=0).astype(BF16)

    for i in range(nh):
        for w, cache in enumerate((k_cache, v_cache)):
            for a, slot in ((h, 1), (1 - h, n + 2 + zz)):
                cs = pl.ds(pl.multiple_of(a * hw + i * HEAD, HEAD), HEAD)
                kv0[slot, i, w] = padded(cache[:, cs].astype(F32)).astype(BF16)
    pl.semaphore_wait(barrier, n - 1 + nt - 1)

    def remote(src, dst, ss, rs, patch):
        return pltpu.make_async_remote_copy(
            src_ref=src,
            dst_ref=dst,
            send_sem=ss,
            recv_sem=rs,
            device_id=(patch, tile),
            device_id_type=MESH,
        )

    def inside_line(z):
        return (z >= 0) & (z < nz)

    def lat_send(di, d):
        step = 1 - 2 * di
        s = zz - step * (d - 1)
        copy = remote(
            lat.at[xx, s], lat.at[xx, s], lz_ss.at[di, d - 1], lz_rs.at[di, d - 1], me + 2 * step
        )
        return inside_line(s) & inside_line(zz + step), copy

    def lat_arrive(di, d):
        step = 1 - 2 * di
        s = zz - step * d
        copy = remote(
            lat.at[xx, s], lat.at[xx, s], lz_ss.at[di, d - 1], lz_rs.at[di, d - 1], me - 2 * step
        )
        return inside_line(s), s, copy

    def lat_cross(s, line):
        return remote(
            lat.at[line, s], lat.at[line, s], lx_ss.at[s], lx_rs.at[s], me + 1 - 2 * xx
        )

    def lat_event(d):
        for di in range(2):
            there, s, copy = lat_arrive(di, d)

            @pl.when(there)
            def _():
                copy.wait_recv()
                if d + 1 < nz:
                    onward, forward = lat_send(di, d + 1)

                    @pl.when(onward)
                    def _():
                        forward.start()

                lat_cross(s, xx).start()

    def slot_of(z, s, a):
        other = 2 * lax.rem(s // 2 - z // 2 + npz, npz) + s % 2
        slot = jnp.where(s == z, 1, jnp.where(s == z + 1 - 2 * (z % 2), n, other))
        return jnp.where(a == z % 2, slot, n + 2 + s)

    def half_of(di, kind):
        return (1 - di) + kind * (2 * di - 1)

    def wanted_at(di, kind, z):
        return (kind == 0) | (z != (nz - 1 if di == 0 else 0))

    def kv_send(di, d, kind, i):
        step = 1 - 2 * di
        s = zz - step * (d - 1)
        a = half_of(di, kind)
        copy = remote(
            kv0.at[slot_of(zz, s, a), i],
            kv0.at[slot_of(zz + step, s, a), i],
            kz_ss.at[di, d - 1, kind, i],
            kz_rs.at[di, d - 1, kind, i],
            me + 2 * step,
        )
        return inside_line(s) & inside_line(zz + step) & wanted_at(di, kind, zz + step), copy

    def kv_cross(s, i, slot):
        return remote(
            kv0.at[slot, i], kv0.at[nz + s, i], kx_ss.at[s, i], kx_rs.at[s, i], me + 1 - 2 * xx
        )

    def event(e):
        d = e // (2 * nh) + 1
        kind = e // nh % 2
        i = e % nh
        for di in range(2):
            step = 1 - 2 * di
            s = zz - step * d
            a = half_of(di, kind)
            slot = slot_of(zz, s, a)

            @pl.when(inside_line(s) & wanted_at(di, kind, zz))
            def _():
                remote(
                    kv0.at[slot, i],
                    kv0.at[slot, i],
                    kz_ss.at[di, d - 1, kind, i],
                    kz_rs.at[di, d - 1, kind, i],
                    me - 2 * step,
                ).wait_recv()
                onward, forward = kv_send(di, d + 1, kind, i)

                @pl.when(onward)
                def _():
                    forward.start()

                @pl.when(a == h)
                def _():
                    kv_cross(s, i, slot).start()

    def start_own(kind, pieces):
        for i in pieces:
            for di in range(2):
                go, copy = kv_send(di, 1, kind, i)

                @pl.when(go)
                def _():
                    copy.start()

    for di in range(2):
        go, copy = lat_send(di, 1)

        @pl.when(go)
        def _():
            copy.start()

    lat_cross(zz, xx).start()
    start_own(0, (0,))
    kv_cross(zz, 0, 1).start()

    lane = lax.broadcasted_iota(jnp.int32, (1, HEAD), 1)
    frequency = jnp.exp(-jnp.log(F32(10000.0)) * (lane % (HEAD // 2)).astype(F32) / (HEAD // 2))
    times = lax.broadcasted_iota(jnp.int32, (HEAD // 2, HEAD), 0).astype(F32)
    angles = times * frequency
    waves = (jnp.cos(angles), jnp.where(lane < HEAD // 2, -1.0, 1.0) * jnp.sin(angles))
    for k, wave in enumerate(waves):
        top = wave.astype(BF16)
        cs = slice(k * HEAD, (k + 1) * HEAD)
        table[0 : HEAD // 2, cs] = top
        table[HEAD // 2 : HEAD, cs] = (wave - top.astype(F32)).astype(BF16)

    waited = set()

    def need(i):
        if i not in waited:
            loads[i].wait()
            waited.add(i)

    def embed(blocks, step):
        count = len(blocks)
        size = count * rows
        vid_b = jnp.concatenate([b[:VID_DEV] for b in blocks], axis=0).astype(BF16)
        aud_b = jnp.concatenate([b[VID_DEV:rows] for b in blocks], axis=0).astype(BF16)
        square = jnp.zeros((size, 1), F32)
        wide = width // 4
        for i in range(4):
            c = slice(i * wide, (i + 1) * wide)
            e = jnp.concatenate([dot(vid_b, w_vid[:, c]), dot(aud_b, w_aud[:, c])], axis=0)
            emb[0:size, c] = e
            square = square + jnp.sum(e * e, axis=1, keepdims=True)
        scale = lax.rsqrt(square / width + EPSILON)
        for i in range(4):
            c = slice(i * wide, (i + 1) * wide)
            x = emb[0:size, c] * scale * (1.0 + mod_scale[step : step + 1, c])
            normed[0:size, c] = (x + mod_shift[step : step + 1, c]).astype(BF16)

    def shard_rows(x, g, count):
        if count == 1:
            return x
        first = count * VID_DEV + g * AUD_DEV
        return jnp.concatenate(
            [x[g * VID_DEV : (g + 1) * VID_DEV], x[first : first + AUD_DEV]], axis=0
        )

    def rotate(x, gain, cos, sin):
        x = x * lax.rsqrt(jnp.mean(x * x, axis=1, keepdims=True) + EPSILON)
        x = x * gain
        return x * cos + pltpu.roll(x, HEAD // 2, 1) * sin

    def gain_row(gain, i):
        return gain[pl.ds(h * nh + i, 1), :]

    def project_kv(count, cos, sin, put):
        raw = dot(normed[0 : count * rows, :], w_qkv[:, 0 : 2 * hw])
        for i in range(nh):
            k = rotate(raw[:, i * HEAD : (i + 1) * HEAD], gain_row(k_gain, i), cos, sin)
            v = raw[:, hw + i * HEAD : hw + (i + 1) * HEAD]
            for g in range(count):
                for w, x in enumerate((k, v)):
                    put(g, i, w, padded(shard_rows(x, g, count)).astype(BF16))

    def project_q(count, cos, sin, targets):
        raw = dot(normed[0 : count * rows, :], w_qkv[:, 2 * hw : 3 * hw])
        for i in range(nh):
            q = rotate(raw[:, i * HEAD : (i + 1) * HEAD], gain_row(q_gain, i), cos, sin)
            for g in range(count):
                q_ref[targets[g], i] = padded(shard_rows(q, g, count)).astype(BF16)

    spot = lax.broadcasted_iota(jnp.int32, (HEAD, 3 * HEAD), 0) % (HEAD // 2)

    def pair_waves(blocks):
        aud = jnp.where(
            lane < AUD_DEV,
            blocks[0][rows + 1 : rows + 2],
            pltpu.roll(blocks[1][rows + 1 : rows + 2], AUD_DEV, 1),
        )
        line = jnp.concatenate([b[rows : rows + 1] for b in blocks] + [aud], axis=1)
        chosen = jnp.where(spot == line.astype(jnp.int32), 1.0, 0.0).astype(BF16)
        both = lax.dot_general(
            chosen, table[...], (((0,), (0,)), ((), ())), preferred_element_type=F32
        )
        pair_cs[0] = both[0 : 2 * rows, 0:HEAD]
        pair_cs[1] = both[0 : 2 * rows, HEAD : 2 * HEAD]

    bw = VID_DEV // (nt * FRAMES * BH)
    gw = bw + 2
    slots = 2 * FRAMES
    row = lax.broadcasted_iota(jnp.int32, (onehot.shape[0], 1), 0)
    f_id = row % slots - 1
    h_id = row // (slots * gw) - 1 + me * BH
    w_id = row // slots % gw - 1 + tile * bw
    inside = (
        (f_id >= 0)
        & (f_id < FRAMES)
        & (h_id >= 0)
        & (h_id < n * BH)
        & (w_id >= 0)
        & (w_id < nt * bw)
    )
    wanted = jnp.where(inside, (f_id * (n * BH) + h_id) * (nt * bw) + w_id, -1)
    for j in range(n):
        c = slice(j * VID_DEV, (j + 1) * VID_DEV)
        onehot[:, c] = jnp.where(cells[:, c] == wanted, 1.0, 0.0).astype(BF16)
    state_out[...] = latents[...]

    lat_event(1)
    start_own(0, range(1, nh))
    for i in range(1, nh):
        kv_cross(zz, i, 1).start()

    own_blocks = [lat[xx, zz].astype(F32), lat[xx, zz + 1 - 2 * h].astype(F32)]
    es = pl.ds(pl.multiple_of(tile * quarter, HEAD), quarter)
    need(0)
    need(1)
    embed(own_blocks, 0)
    embq[...] = padded(
        jnp.concatenate(
            [emb[0:VID_DEV, es], emb[2 * VID_DEV : 2 * VID_DEV + AUD_DEV, es]], axis=0
        )
    )
    if nz > 2:
        lat_event(2)
    start_own(1, range(nh))
    pair_waves(own_blocks)
    for g in range(2):
        for k in range(2):
            cs_ref[g, k] = shard_rows(pair_cs[k], g, 2)

    def put_own(g, i, w, x):
        if g == 0:
            kv0[n + 1, i, w] = x
            kv1[1, i, w] = x
        else:
            kv0[0, i, w] = x
            kv1[n, i, w] = x

    need(2)
    need(3)
    project_kv(2, pair_cs[0], pair_cs[1], put_own)
    for d in range(3, nz):
        lat_event(d)
    need(4)
    project_q(2, pair_cs[0], pair_cs[1], (0, 1))
    for e in range(nh):
        event(e)

    pairs = n // 2
    total_events = (nz - 1) * 2 * nh
    each = -(-(total_events - nh) // (pairs - 1))

    @pl.loop(1, pairs)
    def _(j):
        line = j % 2
        turn = j // 2
        first = 2 * lax.rem(zz // 2 + turn, npz)
        side = jnp.where(line == 0, xx, 1 - xx)

        @pl.when(line == 1)
        def _():
            for g in range(2):
                lat_cross(first + g, 1 - xx).wait_recv()

        blocks = [lat[side, first + g].astype(F32) for g in range(2)]
        embed(blocks, 0)
        base = nh + (j - 1) * each
        for e in range(each // 2):
            event(base + e)
        pair_waves(blocks)
        slot = jnp.where(line == 1, nz + first, 2 * turn)

        def put(g, i, w, x):
            kv1[slot + g, i, w] = x

        project_kv(2, pair_cs[0], pair_cs[1], put)
        for e in range(each // 2, each):
            event(base + e)

    def attend(keys_of, r, first, i):
        keys = keys_of[first : first + n, i, 0].reshape(n * pad, HEAD)
        values = keys_of[first : first + n, i, 1].reshape(n * pad, HEAD)
        scores = lax.dot_general(
            q_ref[r, i], keys, (((1,), (1,)), ((), ())), preferred_element_type=F32
        )
        key_id = lax.broadcasted_iota(jnp.int32, (1, n * pad), 1)
        scores = jnp.where(key_id % pad < rows, scores, -jnp.inf)
        top = jnp.max(scores, axis=1, keepdims=True)
        weights = jnp.exp((scores - top) * HEAD ** (-0.5))
        total = jnp.sum(weights, axis=1, keepdims=True)
        return (dot(weights.astype(BF16), values) / total).astype(BF16)

    for step in range(STEPS):
        state = state_out[...]
        if step > 0:

            def put_fresh(g, i, w, x):
                kv1[n + 1, i, w] = x

            def put_mate(g, i, w, x):
                kv1[0, i, w] = x

            embed([state], step)
            embq[...] = padded(emb[0:rows, es])
            project_kv(1, cs_ref[0, 0], cs_ref[0, 1], put_fresh)
            project_q(1, cs_ref[0, 0], cs_ref[0, 1], (0,))
            remote(p_send, p_recv, p_ss, p_rs, mate).wait_recv()
            embed([p_recv[...].astype(F32)], step)
            project_kv(1, cs_ref[1, 0], cs_ref[1, 1], put_mate)
            project_q(1, cs_ref[1, 0], cs_ref[1, 1], (1,))
        keys_of = kv0 if step == 0 else kv1
        swaps = []
        for i in range(nh):
            if step == 0:
                for s in range(nz):
                    kv_cross(s, i, nz + s).wait_recv()
            o_send[step, i] = attend(keys_of, 1, 0, i)
            copy = remote(
                o_send.at[step, i],
                att.at[step, h, i],
                o_ss.at[step, i],
                o_rs.at[step, i],
                mate,
            )
            copy.start()
            swaps.append(copy)
        for i in range(nh):
            att[step, h, i] = attend(keys_of, 0, 2, i)
        need(5)
        for i in range(nh):
            remote(
                o_send.at[step, i],
                att.at[step, 1 - h, i],
                o_ss.at[step, i],
                o_rs.at[step, i],
                mate,
            ).wait_recv()

        def out_part(owner):
            cs = pl.ds(pl.multiple_of(owner * quarter, HEAD), quarter)
            heads = [att[step, a, i] for a in range(2) for i in range(nh)]
            return dot(jnp.concatenate(heads, axis=1), w_o[:, cs])

        def tile_copy(src, dst, ss, rs, target):
            return pltpu.make_async_remote_copy(
                src_ref=src,
                dst_ref=dst,
                send_sem=ss,
                recv_sem=rs,
                device_id=(me, target),
                device_id_type=MESH,
            )

        sibling = ty * 2 + 1 - core
        first = []
        for j in list(range(1, ny)) + [0]:
            chip = lax.rem(ty + j, ny)
            s1_send[j] = out_part(chip * 2 + 1 - core).astype(BF16)
            copy = tile_copy(
                s1_send.at[j], s1_recv.at[j], s1_ss.at[step, j], s1_rs.at[step, j], sibling
            )
            copy.start()
            first.append((j, copy))
        second = []
        for j, copy in first:
            chip = lax.rem(ty + j, ny)
            mine = out_part(chip * 2 + core)
            copy.wait_recv()
            mine = mine + s1_recv[j].astype(F32)
            if j > 0:
                s2_send[j - 1] = mine.astype(BF16)
                far = tile_copy(
                    s2_send.at[j - 1],
                    s2_recv.at[j - 1],
                    s2_ss.at[step, j],
                    s2_rs.at[step, j],
                    chip * 2 + core,
                )
                far.start()
                second.append((j, far))
            else:
                acc[...] = mine + embq[...]
        for j, far in second:
            far.wait_recv()
            acc[...] += s2_recv[j - 1].astype(F32)
        need(6)
        mixed = acc[0:rows, :]
        square = jnp.sum(mixed * mixed, axis=1, keepdims=True)
        part = dot((mixed * out_gain[:, es]).astype(BF16), w_f[es, :])
        vel_send[0] = jnp.concatenate([part, jnp.broadcast_to(square, (rows, HEAD))], axis=1)
        near = tile_copy(
            vel_send.at[0], vel_recv.at[0], v_ss.at[step, 0], v_rs.at[step, 0], sibling
        )
        near.start()
        near.wait_recv()
        both = vel_send[0] + vel_recv[0]
        vel_send[1] = both
        others = []
        for j in range(1, ny):
            copy = tile_copy(
                vel_send.at[1],
                vel_recv.at[j],
                v_ss.at[step, j],
                v_rs.at[step, j],
                lax.rem(ty + j, ny) * 2 + core,
            )
            copy.start()
            others.append(copy)
        for j, copy in enumerate(others):
            copy.wait_recv()
            both = both + vel_recv[j + 1]
        channels = part.shape[1]
        scale = lax.rsqrt(both[:, channels : channels + 1] / width + EPSILON)
        new_state = state - step_sizes[step] * (both[:, :channels] * scale)
        state_out[...] = new_state
        if step < STEPS - 1:
            p_send[...] = padded(new_state).astype(BF16)
            remote(p_send, p_recv, p_ss, p_rs, mate).start()
        for _, copy in first:
            copy.wait_send()
        for _, copy in second:
            copy.wait_send()
        near.wait_send()
        for copy in others:
            copy.wait_send()
        for copy in swaps:
            copy.wait_send()

    vid[me] = state_out[:VID_DEV, :].astype(BF16)
    sends = []
    for j in list(range(1, n)):
        copy = remote(vid.at[me], vid.at[me], vid_ss.at[j], vid_rs.at[j], lax.rem(me + j, n))
        copy.start()
        sends.append(copy)

    remote(p_send, p_recv, p_ss, p_rs, mate).wait_send()
    for di in range(2):
        for d in range(1, nz):
            go, copy = lat_send(di, d)

            @pl.when(go)
            def _():
                copy.wait_send()

    for s in range(nz):
        lat_cross(s, xx).wait_send()
        for i in range(nh):
            kv_cross(s, i, 1).wait_send()

    @pl.loop(0, total_events)
    def _(e):
        for di in range(2):
            go, copy = kv_send(di, e // (2 * nh) + 1, e // nh % 2, e % nh)

            @pl.when(go)
            def _():
                copy.wait_send()

    need(7)
    for j in range(1, n):
        source = lax.rem(me - j + n, n)
        remote(vid.at[source], vid.at[source], vid_ss.at[j], vid_rs.at[j], source).wait_recv()
    grown[...] = dot(onehot[...], vid[...].reshape(n * VID_DEV, HEAD))
    pieces = []
    for a in range(3):
        for b in range(3):
            for c in range(3):
                starts = [
                    ((h_off + b) * gw + w + c) * slots + a
                    for h_off in range(BH)
                    for w in range(bw)
                ]
                pieces.append(
                    jnp.concatenate([grown[s : s + FRAMES, :] for s in starts], axis=0).astype(BF16)
                )
    total = dot(jnp.concatenate(pieces, axis=1), w_c[...])
    conv_out[...] = (total + conv_b[...]).astype(BF16)
    for copy in sends:
        copy.wait_send()


def local(
    latents,
    timestamps,
    cell_map,
    w_video,
    w_audio,
    mod_scale,
    mod_shift,
    w_query,
    w_key,
    w_value,
    q_gain,
    k_gain,
    k_cache,
    v_cache,
    w_out,
    out_gain,
    w_final,
    step_sizes,
    conv_w,
    conv_b,
):
    n, nt = lax.axis_size("patch"), lax.axis_size("tile")
    rows, channels = latents.shape
    width = w_query.shape[0]
    cols = w_query.shape[1]
    pad = -(-rows // 16) * 16
    quarter = width // nt
    ny = nt // 2
    nz = n // 2
    hw = cols // 2
    nh = hw // HEAD
    bw = VID_DEV // (nt * FRAMES * BH)
    border = (BH + 2) * (bw + 2) * 2 * FRAMES
    cells = FRAMES * BH * bw
    out_ch = conv_w.shape[-1]
    conv_flat = conv_w.reshape(-1, out_ch)
    vmem = pl.BlockSpec(memory_space=pltpu.VMEM)
    hbm = pl.BlockSpec(memory_space=pl.ANY)
    dma = pltpu.SemaphoreType.DMA
    state, conv = pl.pallas_call(
        functools.partial(kernel, n, nt),
        out_shape=(
            jax.ShapeDtypeStruct((rows, channels), F32),
            jax.ShapeDtypeStruct((cells, out_ch), BF16),
        ),
        in_specs=[vmem] * 10 + [pl.BlockSpec(memory_space=pltpu.SMEM), vmem] + [hbm] * 8,
        out_specs=(vmem, vmem),
        scratch_shapes=[
            pltpu.VMEM(w_video.shape, BF16),
            pltpu.VMEM(w_audio.shape, BF16),
            pltpu.VMEM((width, 3 * hw), BF16),
            pltpu.VMEM(w_out.shape, BF16),
            pltpu.VMEM(w_final.shape, BF16),
            pltpu.VMEM(conv_flat.shape, BF16),
            pltpu.VMEM((n + 2 + nz, nh, 2, pad, HEAD), BF16),
            pltpu.VMEM((n + 2, nh, 2, pad, HEAD), BF16),
            pltpu.VMEM((2, nz, pad, HEAD), BF16),
            pltpu.VMEM((2 * rows, width), F32),
            pltpu.VMEM((2 * rows, width), BF16),
            pltpu.VMEM((pad, quarter), F32),
            pltpu.VMEM((2, nh, pad, HEAD), BF16),
            pltpu.VMEM((2, 2, rows, HEAD), F32),
            pltpu.VMEM((2, 2 * rows, HEAD), F32),
            pltpu.VMEM((HEAD, 2 * HEAD), BF16),
            pltpu.VMEM((STEPS, 2, nh, pad, HEAD), BF16),
            pltpu.VMEM((STEPS, nh, pad, HEAD), BF16),
            pltpu.VMEM((pad, HEAD), BF16),
            pltpu.VMEM((pad, HEAD), BF16),
            pltpu.VMEM((pad, quarter), F32),
            pltpu.VMEM((ny, pad, quarter), BF16),
            pltpu.VMEM((ny, pad, quarter), BF16),
            pltpu.VMEM((ny - 1, pad, quarter), BF16),
            pltpu.VMEM((ny - 1, pad, quarter), BF16),
            pltpu.VMEM((2, rows, channels + HEAD), F32),
            pltpu.VMEM((ny, rows, channels + HEAD), F32),
            pltpu.VMEM((n, VID_DEV, channels), BF16),
            pltpu.VMEM((border, n * VID_DEV), BF16),
            pltpu.VMEM((border, channels), F32),
            dma((8,)),
            dma((2, nz - 1)),
            dma((2, nz - 1)),
            dma((nz,)),
            dma((nz,)),
            dma((2, nz - 1, 2, nh)),
            dma((2, nz - 1, 2, nh)),
            dma((nz, nh)),
            dma((nz, nh)),
            dma((STEPS, nh)),
            dma((STEPS, nh)),
            dma(()),
            dma(()),
            dma((STEPS, ny)),
            dma((STEPS, ny)),
            dma((STEPS, ny)),
            dma((STEPS, ny)),
            dma((STEPS, ny)),
            dma((STEPS, ny)),
            dma((n,)),
            dma((n,)),
        ],
        compiler_params=pltpu.CompilerParams(
            collective_id=0, has_side_effects=True, vmem_limit_bytes=63 * 1024 * 1024
        ),
    )(
        latents,
        timestamps.reshape(1, -1),
        cell_map.reshape(1, -1),
        mod_scale,
        mod_shift,
        q_gain.reshape(-1, HEAD),
        k_gain.reshape(-1, HEAD),
        k_cache,
        v_cache,
        out_gain.reshape(1, -1),
        step_sizes,
        conv_b.reshape(1, -1),
        w_video,
        w_audio,
        w_query,
        w_key,
        w_value,
        w_out,
        w_final,
        conv_flat,
    )
    decoded = conv.reshape(BH, bw, FRAMES, out_ch).transpose(2, 0, 1, 3)
    return state, decoded


def solution(mesh):
    return jax.shard_map(
        local,
        mesh=mesh,
        in_specs=(
            P("patch", None),
            P("patch"),
            P(),
            P(),
            P(),
            P(),
            P(),
            P(None, "tile"),
            P(None, "tile"),
            P(None, "tile"),
            P("tile"),
            P("tile"),
            P("patch", "tile"),
            P("patch", "tile"),
            P("tile", None),
            P(),
            P(),
            P(),
            P(),
            P(),
        ),
        out_specs=(P("patch", None), P(None, "patch", "tile", None)),
        check_vma=False,
    )
```

```python
import functools

import jax
import jax.numpy as jnp
from jax import lax
from jax.experimental import pallas as pl
from jax.experimental.pallas import tpu as pltpu
from jax.sharding import PartitionSpec as P

HEAD = 128
VID_DEV = 128
AUD_DEV = 8
STEPS = 2
FRAMES = 8
BH = 2
EPSILON = 1e-06
MESH = pl.DeviceIdType.MESH
F32 = jnp.float32
BF16 = jnp.bfloat16


def dot(a, b):
    return jnp.dot(a, b, preferred_element_type=F32)


def kernel(
    n,
    nt,
    latents,
    stamps,
    cells,
    mod_scale,
    mod_shift,
    q_gain,
    k_gain,
    k_cache,
    v_cache,
    out_gain,
    step_sizes,
    conv_b,
    wv_hbm,
    wa_hbm,
    wq_hbm,
    wk_hbm,
    wval_hbm,
    wo_hbm,
    wf_hbm,
    cw_hbm,
    state_out,
    conv_out,
    w_vid,
    w_aud,
    w_qkv,
    w_o,
    w_f,
    w_c,
    kv0,
    kv1,
    lat,
    emb,
    normed,
    embq,
    q_ref,
    cs_ref,
    pair_cs,
    table,
    att,
    o_send,
    p_send,
    p_recv,
    state_ref,
    st_send,
    st_recv,
    acc,
    s1_send,
    s1_recv,
    s2_send,
    s2_recv,
    vel_send,
    vel_recv,
    vid,
    got,
    sel,
    place,
    grown,
    load_sem,
    lz_ss,
    lz_rs,
    lx_ss,
    lx_rs,
    kz_ss,
    kz_rs,
    kx_ss,
    kx_rs,
    o_ss,
    o_rs,
    p_ss,
    p_rs,
    s1_ss,
    s1_rs,
    s2_ss,
    s2_rs,
    v_ss,
    v_rs,
    vid_ss,
    vid_rs,
):
    rows = latents.shape[0]
    pad = lat.shape[2]
    width = emb.shape[1]
    hw = w_qkv.shape[1] // 3
    nh = hw // HEAD
    part_rows = pad // (nt // 2)
    wing = width // 2
    nz = n // 2
    npz = nz // 2
    me = lax.axis_index("patch")
    tile = lax.axis_index("tile")
    core = tile % 2
    ty = tile // 2
    chunks = acc.shape[0]
    chunk = acc.shape[2]
    zz = me // 2
    xx = me % 2
    h = zz % 2
    mate = me + 2 - 4 * h

    def half_cols(a):
        return pl.ds(pl.multiple_of(a * hw, HEAD), hw)

    loads = []
    for i, (src, dst) in enumerate(
        (
            (wv_hbm, w_vid),
            (wa_hbm, w_aud),
            (wk_hbm.at[:, half_cols(h)], w_qkv.at[:, 0:hw]),
            (wval_hbm.at[:, half_cols(h)], w_qkv.at[:, hw : 2 * hw]),
            (wq_hbm.at[:, half_cols(h)], w_qkv.at[:, 2 * hw : 3 * hw]),
            (wo_hbm, w_o),
            (wf_hbm, w_f),
            (cw_hbm, w_c),
        )
    ):
        copy = pltpu.make_async_copy(src, dst, load_sem.at[i])
        copy.start()
        loads.append(copy)

    got[...] = jnp.zeros(got.shape, BF16)
    barrier = pltpu.get_barrier_semaphore()
    for j in range(1, n):
        pl.semaphore_signal(
            barrier, inc=1, device_id=(lax.rem(me + j, n), tile), device_id_type=MESH
        )
    for j in range(1, nt):
        pl.semaphore_signal(
            barrier, inc=1, device_id=(me, lax.rem(tile + j, nt)), device_id_type=MESH
        )

    def padded(x):
        return jnp.concatenate([x, jnp.zeros((pad - rows, x.shape[1]), F32)], axis=0)

    line_row = lax.broadcasted_iota(jnp.int32, (pad - rows, HEAD), 0)
    aud_stamps = jnp.concatenate(
        [stamps[:, VID_DEV:rows], jnp.zeros((1, HEAD - AUD_DEV), jnp.int32)], axis=1
    ).astype(F32)
    vid_stamps = stamps[:, 0:VID_DEV].astype(F32)
    tail = jnp.where(line_row == 0, vid_stamps, jnp.where(line_row == 1, aud_stamps, 0.0))
    lat[xx, zz] = jnp.concatenate([latents[...], tail], axis=0).astype(BF16)

    def put_kv(where, slot, i, k, v):
        where[slot, i, 0:VID_DEV] = k[:VID_DEV].astype(BF16)
        where[slot, i, VID_DEV : 2 * VID_DEV] = v[:VID_DEV].astype(BF16)
        last = jnp.concatenate([k[VID_DEV:], v[VID_DEV:]], axis=0)
        where[slot, i, 2 * VID_DEV : 2 * rows] = last.astype(BF16)

    for i in range(nh):
        for a, slot in ((h, 1), (1 - h, n + 2 + zz)):
            cs = pl.ds(pl.multiple_of(a * hw + i * HEAD, HEAD), HEAD)
            put_kv(kv0, slot, i, k_cache[:, cs].astype(F32), v_cache[:, cs].astype(F32))
    pl.semaphore_wait(barrier, n - 1 + nt - 1)

    def remote(src, dst, ss, rs, patch):
        return pltpu.make_async_remote_copy(
            src_ref=src,
            dst_ref=dst,
            send_sem=ss,
            recv_sem=rs,
            device_id=(patch, tile),
            device_id_type=MESH,
        )

    def inside_line(z):
        return (z >= 0) & (z < nz)

    def lat_send(di, d):
        step = 1 - 2 * di
        s = zz - step * (d - 1)
        copy = remote(
            lat.at[xx, s], lat.at[xx, s], lz_ss.at[di, d - 1], lz_rs.at[di, d - 1], me + 2 * step
        )
        return inside_line(s) & inside_line(zz + step), copy

    def lat_arrive(di, d):
        step = 1 - 2 * di
        s = zz - step * d
        copy = remote(
            lat.at[xx, s], lat.at[xx, s], lz_ss.at[di, d - 1], lz_rs.at[di, d - 1], me - 2 * step
        )
        return inside_line(s), s, copy

    def lat_cross(s, line):
        return remote(
            lat.at[line, s], lat.at[line, s], lx_ss.at[s], lx_rs.at[s], me + 1 - 2 * xx
        )

    def lat_event(d):
        for di in range(2):
            there, s, copy = lat_arrive(di, d)

            @pl.when(there)
            def _():
                copy.wait_recv()
                if d + 1 < nz:
                    onward, forward = lat_send(di, d + 1)

                    @pl.when(onward)
                    def _():
                        forward.start()

                lat_cross(s, xx).start()

    def slot_of(z, s, a):
        other = 2 * lax.rem(s // 2 - z // 2 + npz, npz) + s % 2
        slot = jnp.where(s == z, 1, jnp.where(s == z + 1 - 2 * (z % 2), n, other))
        return jnp.where(a == z % 2, slot, n + 2 + s)

    def half_of(di, kind):
        return (1 - di) + kind * (2 * di - 1)

    def wanted_at(di, kind, z):
        return (kind == 0) | (z != (nz - 1 if di == 0 else 0))

    def kv_send(di, d, kind, i):
        step = 1 - 2 * di
        s = zz - step * (d - 1)
        a = half_of(di, kind)
        copy = remote(
            kv0.at[slot_of(zz, s, a), i],
            kv0.at[slot_of(zz + step, s, a), i],
            kz_ss.at[di, d - 1, kind, i],
            kz_rs.at[di, d - 1, kind, i],
            me + 2 * step,
        )
        return inside_line(s) & inside_line(zz + step) & wanted_at(di, kind, zz + step), copy

    def kv_cross(s, i, slot):
        return remote(
            kv0.at[slot, i], kv0.at[nz + s, i], kx_ss.at[s, i], kx_rs.at[s, i], me + 1 - 2 * xx
        )

    def event(e):
        d = e // (2 * nh) + 1
        kind = e // nh % 2
        i = e % nh
        for di in range(2):
            step = 1 - 2 * di
            s = zz - step * d
            a = half_of(di, kind)
            slot = slot_of(zz, s, a)

            @pl.when(inside_line(s) & wanted_at(di, kind, zz))
            def _():
                remote(
                    kv0.at[slot, i],
                    kv0.at[slot, i],
                    kz_ss.at[di, d - 1, kind, i],
                    kz_rs.at[di, d - 1, kind, i],
                    me - 2 * step,
                ).wait_recv()
                onward, forward = kv_send(di, d + 1, kind, i)

                @pl.when(onward)
                def _():
                    forward.start()

                @pl.when(a == h)
                def _():
                    kv_cross(s, i, slot).start()

    def start_own(kind, pieces):
        for i in pieces:
            for di in range(2):
                go, copy = kv_send(di, 1, kind, i)

                @pl.when(go)
                def _():
                    copy.start()

    for di in range(2):
        go, copy = lat_send(di, 1)

        @pl.when(go)
        def _():
            copy.start()

    lat_cross(zz, xx).start()
    start_own(0, (0,))
    kv_cross(zz, 0, 1).start()

    lane = lax.broadcasted_iota(jnp.int32, (1, HEAD), 1)
    frequency = jnp.exp(-jnp.log(F32(10000.0)) * (lane % (HEAD // 2)).astype(F32) / (HEAD // 2))
    times = lax.broadcasted_iota(jnp.int32, (HEAD // 2, HEAD), 0).astype(F32)
    angles = times * frequency
    waves = (jnp.cos(angles), jnp.where(lane < HEAD // 2, -1.0, 1.0) * jnp.sin(angles))
    for k, wave in enumerate(waves):
        top = wave.astype(BF16)
        cs = slice(k * HEAD, (k + 1) * HEAD)
        table[0 : HEAD // 2, cs] = top
        table[HEAD // 2 : HEAD, cs] = (wave - top.astype(F32)).astype(BF16)

    waited = set()

    def need(i):
        if i not in waited:
            loads[i].wait()
            waited.add(i)

    def embed(blocks, step):
        count = len(blocks)
        size = count * rows
        vid_b = jnp.concatenate([b[:VID_DEV] for b in blocks], axis=0).astype(BF16)
        aud_b = jnp.concatenate([b[VID_DEV:rows] for b in blocks], axis=0).astype(BF16)
        square = jnp.zeros((size, 1), F32)
        wide = width // 4
        for i in range(4):
            c = slice(i * wide, (i + 1) * wide)
            e = jnp.concatenate([dot(vid_b, w_vid[:, c]), dot(aud_b, w_aud[:, c])], axis=0)
            emb[0:size, c] = e
            square = square + jnp.sum(e * e, axis=1, keepdims=True)
        scale = lax.rsqrt(square / width + EPSILON)
        for i in range(4):
            c = slice(i * wide, (i + 1) * wide)
            x = emb[0:size, c] * scale * (1.0 + mod_scale[step : step + 1, c])
            normed[0:size, c] = (x + mod_shift[step : step + 1, c]).astype(BF16)

    def shard_rows(x, g, count):
        if count == 1:
            return x
        first = count * VID_DEV + g * AUD_DEV
        return jnp.concatenate(
            [x[g * VID_DEV : (g + 1) * VID_DEV], x[first : first + AUD_DEV]], axis=0
        )

    def rotate(x, gain, cos, sin):
        x = x * lax.rsqrt(jnp.mean(x * x, axis=1, keepdims=True) + EPSILON)
        x = x * gain
        return x * cos + pltpu.roll(x, HEAD // 2, 1) * sin

    def gain_row(gain, i):
        return gain[pl.ds(h * nh + i, 1), :]

    def project_kv(count, cos, sin, put):
        raw = dot(normed[0 : count * rows, :], w_qkv[:, 0 : 2 * hw])
        for i in range(nh):
            k = rotate(raw[:, i * HEAD : (i + 1) * HEAD], gain_row(k_gain, i), cos, sin)
            v = raw[:, hw + i * HEAD : hw + (i + 1) * HEAD]
            for g in range(count):
                put(g, i, shard_rows(k, g, count), shard_rows(v, g, count))

    def project_q(count, cos, sin, targets):
        raw = dot(normed[0 : count * rows, :], w_qkv[:, 2 * hw : 3 * hw])
        for i in range(nh):
            q = rotate(raw[:, i * HEAD : (i + 1) * HEAD], gain_row(q_gain, i), cos, sin)
            for g in range(count):
                q_ref[targets[g], i] = padded(shard_rows(q, g, count)).astype(BF16)

    spot = lax.broadcasted_iota(jnp.int32, (HEAD, 3 * HEAD), 0) % (HEAD // 2)

    def pair_waves(blocks):
        aud = jnp.where(
            lane < AUD_DEV,
            blocks[0][rows + 1 : rows + 2],
            pltpu.roll(blocks[1][rows + 1 : rows + 2], AUD_DEV, 1),
        )
        line = jnp.concatenate([b[rows : rows + 1] for b in blocks] + [aud], axis=1)
        chosen = jnp.where(spot == line.astype(jnp.int32), 1.0, 0.0).astype(BF16)
        both = lax.dot_general(
            chosen, table[...], (((0,), (0,)), ((), ())), preferred_element_type=F32
        )
        pair_cs[0] = both[0 : 2 * rows, 0:HEAD]
        pair_cs[1] = both[0 : 2 * rows, HEAD : 2 * HEAD]

    state_ref[...] = padded(latents[...])

    lat_event(1)
    start_own(0, range(1, nh))
    for i in range(1, nh):
        kv_cross(zz, i, 1).start()

    own_blocks = [lat[xx, zz].astype(F32), lat[xx, zz + 1 - 2 * h].astype(F32)]
    es = pl.ds(pl.multiple_of(core * wing, HEAD), wing)
    need(0)
    need(1)
    embed(own_blocks, 0)
    embq[...] = padded(
        jnp.concatenate(
            [emb[0:VID_DEV, es], emb[2 * VID_DEV : 2 * VID_DEV + AUD_DEV, es]], axis=0
        )
    )
    if nz > 2:
        lat_event(2)
    start_own(1, range(nh))
    pair_waves(own_blocks)
    for g in range(2):
        for k in range(2):
            cs_ref[g, k] = shard_rows(pair_cs[k], g, 2)

    def put_own(g, i, k, v):
        put_kv(kv0, n + 1 if g == 0 else 0, i, k, v)
        put_kv(kv1, 1 if g == 0 else n, i, k, v)

    need(2)
    need(3)
    project_kv(2, pair_cs[0], pair_cs[1], put_own)
    for d in range(3, nz):
        lat_event(d)
    need(4)
    project_q(2, pair_cs[0], pair_cs[1], (0, 1))
    for e in range(nh):
        event(e)

    bw = VID_DEV // (nt * FRAMES * BH)
    gw = bw + 2
    slots = 2 * FRAMES
    high, wide_w = n * BH, nt * bw
    share = VID_DEV // (n * nt)
    sent = sel.shape[1]
    room = got.shape[1]
    group = HEAD // room
    row = lax.broadcasted_iota(jnp.int32, (place.shape[0], 1), 0)
    f_id = row % slots - 1
    h_id = row // (slots * gw) - 1 + me * BH
    w_id = row // slots % gw - 1 + tile * bw
    inside = (
        (f_id >= 0)
        & (f_id < FRAMES)
        & (h_id >= 0)
        & (h_id < high)
        & (w_id >= 0)
        & (w_id < wide_w)
    )
    wanted = jnp.where(inside, (f_id * high + h_id) * wide_w + w_id, -1)
    down = lax.broadcasted_iota(jnp.int32, (VID_DEV, VID_DEV), 0)
    along = lax.broadcasted_iota(jnp.int32, (VID_DEV, VID_DEV), 1)

    def block_ranks(cell):
        bh = cell // wide_w % high // BH
        bc = cell % wide_w // bw
        block = (bh * nt + bc).astype(F32)
        column = jnp.sum(jnp.where(down == along, block, 0.0), axis=1, keepdims=True)
        ahead = jnp.where((column == block) & (down < along), 1.0, 0.0)
        return bh, bc, jnp.sum(ahead, axis=0, keepdims=True).astype(jnp.int32)

    def slot_in(ranks, p):
        bh, bc, rank = ranks
        dh = bh - p + 1
        dw = bc - tile + 1
        near_by = (dh >= 0) & (dh < 3) & (dw >= 0) & (dw < 3)
        return jnp.where(near_by, (dh * 3 + dw) * share + rank, -HEAD)

    my_ranks = block_ranks(cells[:, pl.ds(pl.multiple_of(me * VID_DEV, VID_DEV), VID_DEV)])
    pick = lax.broadcasted_iota(jnp.int32, (sent, VID_DEV), 0)
    for j in range(n):
        slot = slot_in(my_ranks, lax.rem(me + j, n))
        sel[j] = jnp.where(pick == slot, 1.0, 0.0).astype(BF16)
    for q in range(n // group):
        found, moved = [], []
        for k in range(group):
            c = slice((q * group + k) * VID_DEV, (q * group + k + 1) * VID_DEV)
            found.append(jnp.where(cells[:, c] == wanted, 1.0, 0.0).astype(BF16))
            slot = slot_in(block_ranks(cells[:, c]), me) + k * room
            moved.append(jnp.where(down == slot, 1.0, 0.0).astype(BF16))
        place[:, q * HEAD : (q + 1) * HEAD] = lax.dot_general(
            jnp.concatenate(found, axis=1),
            jnp.concatenate(moved, axis=1),
            (((1,), (1,)), ((), ())),
            preferred_element_type=F32,
        ).astype(BF16)

    pairs = n // 2
    total_events = (nz - 1) * 2 * nh
    each = -(-(total_events - nh) // (pairs - 1))

    @pl.loop(1, pairs)
    def _(j):
        line = j % 2
        turn = j // 2
        first = 2 * lax.rem(zz // 2 + turn, npz)
        side = jnp.where(line == 0, xx, 1 - xx)

        @pl.when(line == 1)
        def _():
            for g in range(2):
                lat_cross(first + g, 1 - xx).wait_recv()

        blocks = [lat[side, first + g].astype(F32) for g in range(2)]
        embed(blocks, 0)
        base = nh + (j - 1) * each
        for e in range(each // 2):
            event(base + e)
        pair_waves(blocks)
        slot = jnp.where(line == 1, nz + first, 2 * turn)

        def put(g, i, k, v):
            put_kv(kv1, slot + g, i, k, v)

        project_kv(2, pair_cs[0], pair_cs[1], put)
        for e in range(each // 2, each):
            event(base + e)

    def attend(keys_of, r, first, i):
        span = slice(first, first + n)
        last = keys_of[span, i, 2 * VID_DEV : 2 * rows].astype(F32)
        last_keys = last[:, :AUD_DEV].reshape(n * AUD_DEV, HEAD).astype(BF16)
        last_values = last[:, AUD_DEV:].reshape(n * AUD_DEV, HEAD).astype(BF16)
        keys = jnp.concatenate(
            [keys_of[span, i, 0:VID_DEV].reshape(n * VID_DEV, HEAD), last_keys], axis=0
        )
        values = jnp.concatenate(
            [keys_of[span, i, VID_DEV : 2 * VID_DEV].reshape(n * VID_DEV, HEAD), last_values],
            axis=0,
        )
        scores = lax.dot_general(
            q_ref[r, i], keys, (((1,), (1,)), ((), ())), preferred_element_type=F32
        )
        top = jnp.max(scores, axis=1, keepdims=True)
        weights = jnp.exp((scores - top) * HEAD ** (-0.5))
        total = jnp.sum(weights, axis=1, keepdims=True)
        return (dot(weights.astype(BF16), values) / total).astype(BF16)

    for step in range(STEPS):
        state = state_ref[...]
        if step > 0:

            def put_fresh(g, i, k, v):
                put_kv(kv1, n + 1, i, k, v)

            def put_mate(g, i, k, v):
                put_kv(kv1, 0, i, k, v)

            embed([state], step)
            embq[...] = padded(emb[0:rows, es])
            project_kv(1, cs_ref[0, 0], cs_ref[0, 1], put_fresh)
            project_q(1, cs_ref[0, 0], cs_ref[0, 1], (0,))
            remote(p_send, p_recv, p_ss, p_rs, mate).wait_recv()
            embed([p_recv[...].astype(F32)], step)
            project_kv(1, cs_ref[1, 0], cs_ref[1, 1], put_mate)
            project_q(1, cs_ref[1, 0], cs_ref[1, 1], (1,))
        keys_of = kv0 if step == 0 else kv1
        swaps = []
        for i in range(nh):
            if step == 0:
                for s in range(nz):
                    kv_cross(s, i, nz + s).wait_recv()
            o_send[step, i] = attend(keys_of, 1, 0, i)
            copy = remote(
                o_send.at[step, i],
                att.at[step, h, i],
                o_ss.at[step, i],
                o_rs.at[step, i],
                mate,
            )
            copy.start()
            swaps.append(copy)
        for i in range(nh):
            att[step, h, i] = attend(keys_of, 0, 2, i)
        need(5)
        for i in range(nh):
            remote(
                o_send.at[step, i],
                att.at[step, 1 - h, i],
                o_ss.at[step, i],
                o_rs.at[step, i],
                mate,
            ).wait_recv()

        heads = [att[step, a, i] for a in range(2) for i in range(nh)]
        whole = jnp.concatenate(heads, axis=1).astype(F32)
        turned = jnp.concatenate([whole[part_rows:], whole[:part_rows]], axis=0)
        mine_att = jnp.where(ty == 0, turned, whole).astype(BF16)

        def out_part(side, k):
            cs = pl.ds(pl.multiple_of(side * wing + k * chunk, HEAD), chunk)
            return dot(mine_att, w_o[:, cs])

        def tile_copy(src, dst, ss, rs, target):
            return pltpu.make_async_remote_copy(
                src_ref=src,
                dst_ref=dst,
                send_sem=ss,
                recv_sem=rs,
                device_id=(me, target),
                device_id_type=MESH,
            )

        sibling = ty * 2 + 1 - core
        across = (1 - ty) * 2 + core
        near_rows = pl.ds(pl.multiple_of(ty * part_rows, 8), part_rows)
        first = []
        for k in range(chunks):
            s1_send[k] = out_part(1 - core, k).astype(BF16)
            copy = tile_copy(
                s1_send.at[k], s1_recv.at[k], s1_ss.at[step, k], s1_rs.at[step, k], sibling
            )
            copy.start()
            first.append(copy)
        second = []
        far_parts = []
        for k in range(chunks):
            mine = out_part(core, k)
            first[k].wait_recv()
            mine = mine + s1_recv[k].astype(F32)
            far_parts.append(mine[:part_rows])
            ks = pl.ds(k * chunk, chunk)
            acc[k] = mine[part_rows:] + embq[near_rows, ks]
            if k % 2 == 1:
                j = k // 2
                s2_send[j] = jnp.concatenate(far_parts, axis=0).astype(BF16)
                far_parts = []
                far = tile_copy(
                    s2_send.at[j], s2_recv.at[j], s2_ss.at[step, j], s2_rs.at[step, j], across
                )
                far.start()
                second.append(far)
        need(6)
        square = jnp.zeros((part_rows, 1), F32)
        part = jnp.zeros((part_rows, w_f.shape[1]), F32)
        for j, far in enumerate(second):
            far.wait_recv()
            came = s2_recv[j].astype(F32)
            for half in range(2):
                k = 2 * j + half
                mixed = acc[k] + came[half * part_rows : (half + 1) * part_rows]
                square = square + jnp.sum(mixed * mixed, axis=1, keepdims=True)
                fs = pl.ds(pl.multiple_of(core * wing + k * chunk, HEAD), chunk)
                part = part + dot((mixed * out_gain[:, fs]).astype(BF16), w_f[fs, :])
        channels = part.shape[1]
        vel_send[...] = jnp.concatenate(
            [part, jnp.broadcast_to(square, (part_rows, HEAD))], axis=1
        )
        near = tile_copy(vel_send, vel_recv, v_ss.at[step, 0], v_rs.at[step, 0], sibling)
        near.start()
        near.wait_recv()
        both = vel_send[...] + vel_recv[...]
        scale = lax.rsqrt(both[:, channels : channels + 1] / width + EPSILON)
        fresh = state_ref[near_rows, :] - step_sizes[step] * (both[:, :channels] * scale)
        st_send[...] = fresh
        over = tile_copy(st_send, st_recv.at[step], v_ss.at[step, 1], v_rs.at[step, 1], across)
        over.start()
        over.wait_recv()
        other = st_recv[step]
        new_state = jnp.concatenate(
            [jnp.where(ty == 0, fresh, other), jnp.where(ty == 0, other, fresh)], axis=0
        )
        state_ref[...] = new_state
        if step < STEPS - 1:
            p_send[...] = new_state.astype(BF16)
            remote(p_send, p_recv, p_ss, p_rs, mate).start()
        for copy in first + second + [near, over] + swaps:
            copy.wait_send()

    mine = dot(sel[...].reshape(n * sent, VID_DEV), state_ref[0:VID_DEV, :].astype(BF16))
    vid[...] = mine.astype(BF16).reshape(n, sent, HEAD)
    sends = []
    for j in range(1, n):
        copy = remote(
            vid.at[j], got.at[me, 0:sent], vid_ss.at[j], vid_rs.at[j], lax.rem(me + j, n)
        )
        copy.start()
        sends.append(copy)
    got[me, 0:sent] = vid[0]
    state_out[...] = state_ref[0:rows, :]

    remote(p_send, p_recv, p_ss, p_rs, mate).wait_send()
    for di in range(2):
        for d in range(1, nz):
            go, copy = lat_send(di, d)

            @pl.when(go)
            def _():
                copy.wait_send()

    for s in range(nz):
        lat_cross(s, xx).wait_send()
        for i in range(nh):
            kv_cross(s, i, 1).wait_send()

    @pl.loop(0, total_events)
    def _(e):
        for di in range(2):
            go, copy = kv_send(di, e // (2 * nh) + 1, e // nh % 2, e % nh)

            @pl.when(go)
            def _():
                copy.wait_send()

    need(7)
    for j in range(1, n):
        source = lax.rem(me - j + n, n)
        landed = got.at[source, 0:sent]
        remote(vid.at[j], landed, vid_ss.at[j], vid_rs.at[j], source).wait_recv()
    grown[...] = dot(place[...], got[...].reshape(n * room, HEAD))
    pieces = []
    for a in range(3):
        for b in range(3):
            for c in range(3):
                starts = [
                    ((h_off + b) * gw + w + c) * slots + a
                    for h_off in range(BH)
                    for w in range(bw)
                ]
                pieces.append(
                    jnp.concatenate([grown[s : s + FRAMES, :] for s in starts], axis=0).astype(BF16)
                )
    total = dot(jnp.concatenate(pieces, axis=1), w_c[...])
    conv_out[...] = (total + conv_b[...]).astype(BF16)
    for copy in sends:
        copy.wait_send()


def local(
    latents,
    timestamps,
    cell_map,
    w_video,
    w_audio,
    mod_scale,
    mod_shift,
    w_query,
    w_key,
    w_value,
    q_gain,
    k_gain,
    k_cache,
    v_cache,
    w_out,
    out_gain,
    w_final,
    step_sizes,
    conv_w,
    conv_b,
):
    n, nt = lax.axis_size("patch"), lax.axis_size("tile")
    rows, channels = latents.shape
    width = w_query.shape[0]
    cols = w_query.shape[1]
    pad = -(-rows // 16) * 16
    part_rows = pad // (nt // 2)
    wing = width // 2
    chunk = 256
    chunks = wing // chunk
    nz = n // 2
    hw = cols // 2
    nh = hw // HEAD
    bw = VID_DEV // (nt * FRAMES * BH)
    border = (BH + 2) * (bw + 2) * 2 * FRAMES
    cells = FRAMES * BH * bw
    sent = -(-9 * VID_DEV // (n * nt * 16)) * 16
    room = next(r for r in (16, 32, 64, 128) if r >= sent)
    out_ch = conv_w.shape[-1]
    conv_flat = conv_w.reshape(-1, out_ch)
    vmem = pl.BlockSpec(memory_space=pltpu.VMEM)
    hbm = pl.BlockSpec(memory_space=pl.ANY)
    dma = pltpu.SemaphoreType.DMA
    state, conv = pl.pallas_call(
        functools.partial(kernel, n, nt),
        out_shape=(
            jax.ShapeDtypeStruct((rows, channels), F32),
            jax.ShapeDtypeStruct((cells, out_ch), BF16),
        ),
        in_specs=[vmem] * 10 + [pl.BlockSpec(memory_space=pltpu.SMEM), vmem] + [hbm] * 8,
        out_specs=(vmem, vmem),
        scratch_shapes=[
            pltpu.VMEM(w_video.shape, BF16),
            pltpu.VMEM(w_audio.shape, BF16),
            pltpu.VMEM((width, 3 * hw), BF16),
            pltpu.VMEM(w_out.shape, BF16),
            pltpu.VMEM(w_final.shape, BF16),
            pltpu.VMEM(conv_flat.shape, BF16),
            pltpu.VMEM((n + 2 + nz, nh, 2 * rows, HEAD), BF16),
            pltpu.VMEM((n + 2, nh, 2 * rows, HEAD), BF16),
            pltpu.VMEM((2, nz, pad, HEAD), BF16),
            pltpu.VMEM((2 * rows, width), F32),
            pltpu.VMEM((2 * rows, width), BF16),
            pltpu.VMEM((pad, wing), F32),
            pltpu.VMEM((2, nh, pad, HEAD), BF16),
            pltpu.VMEM((2, 2, rows, HEAD), F32),
            pltpu.VMEM((2, 2 * rows, HEAD), F32),
            pltpu.VMEM((HEAD, 2 * HEAD), BF16),
            pltpu.VMEM((STEPS, 2, nh, pad, HEAD), BF16),
            pltpu.VMEM((STEPS, nh, pad, HEAD), BF16),
            pltpu.VMEM((pad, HEAD), BF16),
            pltpu.VMEM((pad, HEAD), BF16),
            pltpu.VMEM((pad, channels), F32),
            pltpu.VMEM((part_rows, channels), F32),
            pltpu.VMEM((STEPS, part_rows, channels), F32),
            pltpu.VMEM((chunks, part_rows, chunk), F32),
            pltpu.VMEM((chunks, pad, chunk), BF16),
            pltpu.VMEM((chunks, pad, chunk), BF16),
            pltpu.VMEM((chunks // 2, pad, chunk), BF16),
            pltpu.VMEM((chunks // 2, pad, chunk), BF16),
            pltpu.VMEM((part_rows, channels + HEAD), F32),
            pltpu.VMEM((part_rows, channels + HEAD), F32),
            pltpu.VMEM((n, sent, channels), BF16),
            pltpu.VMEM((n, room, channels), BF16),
            pltpu.VMEM((n, sent, VID_DEV), BF16),
            pltpu.VMEM((border, n * room), BF16),
            pltpu.VMEM((border, channels), F32),
            dma((8,)),
            dma((2, nz - 1)),
            dma((2, nz - 1)),
            dma((nz,)),
            dma((nz,)),
            dma((2, nz - 1, 2, nh)),
            dma((2, nz - 1, 2, nh)),
            dma((nz, nh)),
            dma((nz, nh)),
            dma((STEPS, nh)),
            dma((STEPS, nh)),
            dma(()),
            dma(()),
            dma((STEPS, chunks)),
            dma((STEPS, chunks)),
            dma((STEPS, chunks // 2)),
            dma((STEPS, chunks // 2)),
            dma((STEPS, 2)),
            dma((STEPS, 2)),
            dma((n,)),
            dma((n,)),
        ],
        compiler_params=pltpu.CompilerParams(
            collective_id=0, has_side_effects=True, vmem_limit_bytes=63 * 1024 * 1024
        ),
    )(
        latents,
        timestamps.reshape(1, -1),
        cell_map.reshape(1, -1),
        mod_scale,
        mod_shift,
        q_gain.reshape(-1, HEAD),
        k_gain.reshape(-1, HEAD),
        k_cache,
        v_cache,
        out_gain.reshape(1, -1),
        step_sizes,
        conv_b.reshape(1, -1),
        w_video,
        w_audio,
        w_query,
        w_key,
        w_value,
        w_out,
        w_final,
        conv_flat,
    )
    decoded = conv.reshape(BH, bw, FRAMES, out_ch).transpose(2, 0, 1, 3)
    return state, decoded


def solution(mesh):
    return jax.shard_map(
        local,
        mesh=mesh,
        in_specs=(
            P("patch", None),
            P("patch"),
            P(),
            P(),
            P(),
            P(),
            P(),
            P(None, "tile"),
            P(None, "tile"),
            P(None, "tile"),
            P("tile"),
            P("tile"),
            P("patch", "tile"),
            P("patch", "tile"),
            P("tile", None),
            P(),
            P(),
            P(),
            P(),
            P(),
        ),
        out_specs=(P("patch", None), P(None, "patch", "tile", None)),
        check_vma=False,
    )
```

```python
import functools

import jax
import jax.numpy as jnp
from jax import lax
from jax.experimental import pallas as pl
from jax.experimental.pallas import tpu as pltpu
from jax.sharding import PartitionSpec as P

HEAD = 128
VID_DEV = 128
AUD_DEV = 8
STEPS = 2
FRAMES = 8
BH = 2
EPSILON = 1e-06
MESH = pl.DeviceIdType.MESH
F32 = jnp.float32
BF16 = jnp.bfloat16


def dot(a, b):
    return jnp.dot(a, b, preferred_element_type=F32)


def kernel(
    n,
    nt,
    latents,
    stamps,
    cells,
    mod_scale,
    mod_shift,
    q_gain,
    k_gain,
    k_cache,
    v_cache,
    out_gain,
    step_sizes,
    conv_b,
    wv_hbm,
    wa_hbm,
    wq_hbm,
    wk_hbm,
    wval_hbm,
    wo_hbm,
    wf_hbm,
    cw_hbm,
    state_out,
    conv_out,
    w_vid,
    w_aud,
    w_qkv,
    w_o,
    w_f,
    w_c,
    kv0,
    kv1,
    lat,
    emb,
    normed,
    embq,
    q_ref,
    cs_ref,
    pair_cs,
    table,
    att,
    o_send,
    p_send,
    p_recv,
    state_ref,
    st_send,
    st_recv,
    acc,
    s1_send,
    s1_recv,
    s2_send,
    s2_recv,
    vel_send,
    vel_recv,
    vid,
    got,
    sel,
    place,
    grown,
    load_sem,
    lz_ss,
    lz_rs,
    lx_ss,
    lx_rs,
    kz_ss,
    kz_rs,
    kx_ss,
    kx_rs,
    o_ss,
    o_rs,
    p_ss,
    p_rs,
    s1_ss,
    s1_rs,
    s2_ss,
    s2_rs,
    v_ss,
    v_rs,
    vid_ss,
    vid_rs,
):
    rows = latents.shape[0]
    pad = lat.shape[2]
    width = emb.shape[1]
    hw = w_qkv.shape[1] // 3
    nh = hw // HEAD
    part_rows = pad // (nt // 2)
    wing = width // 2
    nz = n // 2
    npz = nz // 2
    me = lax.axis_index("patch")
    tile = lax.axis_index("tile")
    core = tile % 2
    ty = tile // 2
    chunks = acc.shape[0]
    chunk = acc.shape[2]
    zz = me // 2
    xx = me % 2
    h = zz % 2
    mate = me + 2 - 4 * h

    def half_cols(a):
        return pl.ds(pl.multiple_of(a * hw, HEAD), hw)

    loads = []
    for i, (src, dst) in enumerate(
        (
            (wv_hbm, w_vid),
            (wa_hbm, w_aud),
            (wk_hbm.at[:, half_cols(h)], w_qkv.at[:, 0:hw]),
            (wval_hbm.at[:, half_cols(h)], w_qkv.at[:, hw : 2 * hw]),
            (wq_hbm.at[:, half_cols(h)], w_qkv.at[:, 2 * hw : 3 * hw]),
            (wo_hbm, w_o),
            (wf_hbm, w_f),
            (cw_hbm, w_c),
        )
    ):
        copy = pltpu.make_async_copy(src, dst, load_sem.at[i])
        copy.start()
        loads.append(copy)

    got[...] = jnp.zeros(got.shape, BF16)
    barrier = pltpu.get_barrier_semaphore()
    for z, z_there in ((-1, zz > 0), (1, zz < nz - 1)):

        @pl.when(z_there)
        def _():
            pl.semaphore_signal(
                barrier, inc=1, device_id=(me + 2 * z, tile), device_id_type=MESH
            )

    sibling = ty * 2 + 1 - core
    across = (1 - ty) * 2 + core
    for spot in ((me + 1 - 2 * xx, tile), (me, sibling), (me, across)):
        pl.semaphore_signal(barrier, inc=1, device_id=spot, device_id_type=MESH)

    def padded(x):
        return jnp.concatenate([x, jnp.zeros((pad - rows, x.shape[1]), F32)], axis=0)

    line_row = lax.broadcasted_iota(jnp.int32, (pad - rows, HEAD), 0)
    aud_stamps = jnp.concatenate(
        [stamps[:, VID_DEV:rows], jnp.zeros((1, HEAD - AUD_DEV), jnp.int32)], axis=1
    ).astype(F32)
    vid_stamps = stamps[:, 0:VID_DEV].astype(F32)
    tail = jnp.where(line_row == 0, vid_stamps, jnp.where(line_row == 1, aud_stamps, 0.0))
    lat[xx, zz] = jnp.concatenate([latents[...], tail], axis=0).astype(BF16)

    def put_kv(where, slot, i, k, v):
        where[slot, i, 0:VID_DEV] = k[:VID_DEV].astype(BF16)
        where[slot, i, VID_DEV : 2 * VID_DEV] = v[:VID_DEV].astype(BF16)
        last = jnp.concatenate([k[VID_DEV:], v[VID_DEV:]], axis=0)
        where[slot, i, 2 * VID_DEV : 2 * rows] = last.astype(BF16)

    for i in range(nh):
        for a, slot in ((h, 1), (1 - h, n + 2 + zz)):
            cs = pl.ds(pl.multiple_of(a * hw + i * HEAD, HEAD), HEAD)
            put_kv(kv0, slot, i, k_cache[:, cs].astype(F32), v_cache[:, cs].astype(F32))
    pl.semaphore_wait(barrier, 5 - jnp.where((zz == 0) | (zz == nz - 1), 1, 0))

    def remote(src, dst, ss, rs, patch):
        return pltpu.make_async_remote_copy(
            src_ref=src,
            dst_ref=dst,
            send_sem=ss,
            recv_sem=rs,
            device_id=(patch, tile),
            device_id_type=MESH,
        )

    def inside_line(z):
        return (z >= 0) & (z < nz)

    def lat_send(di, d):
        step = 1 - 2 * di
        s = zz - step * (d - 1)
        copy = remote(
            lat.at[xx, s], lat.at[xx, s], lz_ss.at[di, d - 1], lz_rs.at[di, d - 1], me + 2 * step
        )
        return inside_line(s) & inside_line(zz + step), copy

    def lat_arrive(di, d):
        step = 1 - 2 * di
        s = zz - step * d
        copy = remote(
            lat.at[xx, s], lat.at[xx, s], lz_ss.at[di, d - 1], lz_rs.at[di, d - 1], me - 2 * step
        )
        return inside_line(s), s, copy

    def lat_cross(s, line):
        return remote(
            lat.at[line, s], lat.at[line, s], lx_ss.at[s], lx_rs.at[s], me + 1 - 2 * xx
        )

    def lat_event(d):
        for di in range(2):
            there, s, copy = lat_arrive(di, d)

            @pl.when(there)
            def _():
                copy.wait_recv()
                if d + 1 < nz:
                    onward, forward = lat_send(di, d + 1)

                    @pl.when(onward)
                    def _():
                        forward.start()

                lat_cross(s, xx).start()

    def slot_of(z, s, a):
        other = 2 * lax.rem(s // 2 - z // 2 + npz, npz) + s % 2
        slot = jnp.where(s == z, 1, jnp.where(s == z + 1 - 2 * (z % 2), n, other))
        return jnp.where(a == z % 2, slot, n + 2 + s)

    def half_of(di, kind):
        return (1 - di) + kind * (2 * di - 1)

    def wanted_at(di, kind, z):
        return (kind == 0) | (z != (nz - 1 if di == 0 else 0))

    def kv_send(di, d, kind, i):
        step = 1 - 2 * di
        s = zz - step * (d - 1)
        a = half_of(di, kind)
        copy = remote(
            kv0.at[slot_of(zz, s, a), i],
            kv0.at[slot_of(zz + step, s, a), i],
            kz_ss.at[di, d - 1, kind, i],
            kz_rs.at[di, d - 1, kind, i],
            me + 2 * step,
        )
        return inside_line(s) & inside_line(zz + step) & wanted_at(di, kind, zz + step), copy

    def kv_cross(s, i, slot):
        return remote(
            kv0.at[slot, i], kv0.at[nz + s, i], kx_ss.at[s, i], kx_rs.at[s, i], me + 1 - 2 * xx
        )

    def event(e):
        d = e // (2 * nh) + 1
        kind = e // nh % 2
        i = e % nh
        for di in range(2):
            step = 1 - 2 * di
            s = zz - step * d
            a = half_of(di, kind)
            slot = slot_of(zz, s, a)

            @pl.when(inside_line(s) & wanted_at(di, kind, zz))
            def _():
                remote(
                    kv0.at[slot, i],
                    kv0.at[slot, i],
                    kz_ss.at[di, d - 1, kind, i],
                    kz_rs.at[di, d - 1, kind, i],
                    me - 2 * step,
                ).wait_recv()
                onward, forward = kv_send(di, d + 1, kind, i)

                @pl.when(onward)
                def _():
                    forward.start()

                @pl.when(a == h)
                def _():
                    kv_cross(s, i, slot).start()

    def start_own(kind, pieces):
        for i in pieces:
            for di in range(2):
                go, copy = kv_send(di, 1, kind, i)

                @pl.when(go)
                def _():
                    copy.start()

    for di in range(2):
        go, copy = lat_send(di, 1)

        @pl.when(go)
        def _():
            copy.start()

    lat_cross(zz, xx).start()
    start_own(0, (0,))
    kv_cross(zz, 0, 1).start()

    lane = lax.broadcasted_iota(jnp.int32, (1, HEAD), 1)
    frequency = jnp.exp(-jnp.log(F32(10000.0)) * (lane % (HEAD // 2)).astype(F32) / (HEAD // 2))
    times = lax.broadcasted_iota(jnp.int32, (HEAD // 2, HEAD), 0).astype(F32)
    angles = times * frequency
    waves = (jnp.cos(angles), jnp.where(lane < HEAD // 2, -1.0, 1.0) * jnp.sin(angles))
    for k, wave in enumerate(waves):
        top = wave.astype(BF16)
        cs = slice(k * HEAD, (k + 1) * HEAD)
        table[0 : HEAD // 2, cs] = top
        table[HEAD // 2 : HEAD, cs] = (wave - top.astype(F32)).astype(BF16)

    waited = set()

    def need(i):
        if i not in waited:
            loads[i].wait()
            waited.add(i)

    def embed(blocks, step):
        count = len(blocks)
        size = count * rows
        vid_b = jnp.concatenate([b[:VID_DEV] for b in blocks], axis=0).astype(BF16)
        aud_b = jnp.concatenate([b[VID_DEV:rows] for b in blocks], axis=0).astype(BF16)
        square = jnp.zeros((size, 1), F32)
        wide = width // 4
        for i in range(4):
            c = slice(i * wide, (i + 1) * wide)
            e = jnp.concatenate([dot(vid_b, w_vid[:, c]), dot(aud_b, w_aud[:, c])], axis=0)
            emb[0:size, c] = e
            square = square + jnp.sum(e * e, axis=1, keepdims=True)
        scale = lax.rsqrt(square / width + EPSILON)
        for i in range(4):
            c = slice(i * wide, (i + 1) * wide)
            x = emb[0:size, c] * scale * (1.0 + mod_scale[step : step + 1, c])
            normed[0:size, c] = (x + mod_shift[step : step + 1, c]).astype(BF16)

    def shard_rows(x, g, count):
        if count == 1:
            return x
        first = count * VID_DEV + g * AUD_DEV
        return jnp.concatenate(
            [x[g * VID_DEV : (g + 1) * VID_DEV], x[first : first + AUD_DEV]], axis=0
        )

    def rotate(x, gain, cos, sin):
        x = x * lax.rsqrt(jnp.mean(x * x, axis=1, keepdims=True) + EPSILON)
        x = x * gain
        return x * cos + pltpu.roll(x, HEAD // 2, 1) * sin

    def gain_row(gain, i):
        return gain[pl.ds(h * nh + i, 1), :]

    def project_kv(count, cos, sin, put):
        raw = dot(normed[0 : count * rows, :], w_qkv[:, 0 : 2 * hw])
        for i in range(nh):
            k = rotate(raw[:, i * HEAD : (i + 1) * HEAD], gain_row(k_gain, i), cos, sin)
            v = raw[:, hw + i * HEAD : hw + (i + 1) * HEAD]
            for g in range(count):
                put(g, i, shard_rows(k, g, count), shard_rows(v, g, count))

    def project_q(count, cos, sin, targets):
        raw = dot(normed[0 : count * rows, :], w_qkv[:, 2 * hw : 3 * hw])
        for i in range(nh):
            q = rotate(raw[:, i * HEAD : (i + 1) * HEAD], gain_row(q_gain, i), cos, sin)
            for g in range(count):
                q_ref[targets[g], i] = padded(shard_rows(q, g, count)).astype(BF16)

    spot = lax.broadcasted_iota(jnp.int32, (HEAD, 3 * HEAD), 0) % (HEAD // 2)

    def pair_waves(blocks):
        aud = jnp.where(
            lane < AUD_DEV,
            blocks[0][rows + 1 : rows + 2],
            pltpu.roll(blocks[1][rows + 1 : rows + 2], AUD_DEV, 1),
        )
        line = jnp.concatenate([b[rows : rows + 1] for b in blocks] + [aud], axis=1)
        chosen = jnp.where(spot == line.astype(jnp.int32), 1.0, 0.0).astype(BF16)
        both = lax.dot_general(
            chosen, table[...], (((0,), (0,)), ((), ())), preferred_element_type=F32
        )
        pair_cs[0] = both[0 : 2 * rows, 0:HEAD]
        pair_cs[1] = both[0 : 2 * rows, HEAD : 2 * HEAD]

    state_ref[...] = padded(latents[...])

    lat_event(1)
    start_own(0, range(1, nh))
    for i in range(1, nh):
        kv_cross(zz, i, 1).start()

    own_blocks = [lat[xx, zz].astype(F32), lat[xx, zz + 1 - 2 * h].astype(F32)]
    es = pl.ds(pl.multiple_of(core * wing, HEAD), wing)
    need(0)
    need(1)
    embed(own_blocks, 0)
    embq[...] = padded(
        jnp.concatenate(
            [emb[0:VID_DEV, es], emb[2 * VID_DEV : 2 * VID_DEV + AUD_DEV, es]], axis=0
        )
    )
    if nz > 2:
        lat_event(2)
    start_own(1, range(nh))
    pair_waves(own_blocks)
    for g in range(2):
        for k in range(2):
            cs_ref[g, k] = shard_rows(pair_cs[k], g, 2)

    def put_own(g, i, k, v):
        put_kv(kv0, n + 1 if g == 0 else 0, i, k, v)
        put_kv(kv1, 1 if g == 0 else n, i, k, v)

    need(2)
    need(3)
    project_kv(2, pair_cs[0], pair_cs[1], put_own)
    for d in range(3, nz):
        lat_event(d)
    need(4)
    project_q(2, pair_cs[0], pair_cs[1], (0, 1))
    for e in range(nh):
        event(e)

    bw = VID_DEV // (nt * FRAMES * BH)
    gw = bw + 2
    slots = 2 * FRAMES
    high, wide_w = n * BH, nt * bw
    share = VID_DEV // (n * nt)
    sent = sel.shape[1]
    room = got.shape[1]
    group = HEAD // room
    row = lax.broadcasted_iota(jnp.int32, (place.shape[0], 1), 0)
    f_id = row % slots - 1
    h_id = row // (slots * gw) - 1 + me * BH
    w_id = row // slots % gw - 1 + tile * bw
    inside = (
        (f_id >= 0)
        & (f_id < FRAMES)
        & (h_id >= 0)
        & (h_id < high)
        & (w_id >= 0)
        & (w_id < wide_w)
    )
    wanted = jnp.where(inside, (f_id * high + h_id) * wide_w + w_id, -1)
    down = lax.broadcasted_iota(jnp.int32, (VID_DEV, VID_DEV), 0)
    along = lax.broadcasted_iota(jnp.int32, (VID_DEV, VID_DEV), 1)

    def block_ranks(cell):
        bh = cell // wide_w % high // BH
        bc = cell % wide_w // bw
        block = (bh * nt + bc).astype(F32)
        column = jnp.sum(jnp.where(down == along, block, 0.0), axis=1, keepdims=True)
        ahead = jnp.where((column == block) & (down < along), 1.0, 0.0)
        return bh, bc, jnp.sum(ahead, axis=0, keepdims=True).astype(jnp.int32)

    def slot_in(ranks, p):
        bh, bc, rank = ranks
        dh = bh - p + 1
        dw = bc - tile + 1
        near_by = (dh >= 0) & (dh < 3) & (dw >= 0) & (dw < 3)
        return jnp.where(near_by, (dh * 3 + dw) * share + rank, -HEAD)

    my_ranks = block_ranks(cells[:, pl.ds(pl.multiple_of(me * VID_DEV, VID_DEV), VID_DEV)])
    pick = lax.broadcasted_iota(jnp.int32, (sent, VID_DEV), 0)
    for j in range(n):
        slot = slot_in(my_ranks, lax.rem(me + j, n))
        sel[j] = jnp.where(pick == slot, 1.0, 0.0).astype(BF16)
    for q in range(n // group):
        found, moved = [], []
        for k in range(group):
            c = slice((q * group + k) * VID_DEV, (q * group + k + 1) * VID_DEV)
            found.append(jnp.where(cells[:, c] == wanted, 1.0, 0.0).astype(BF16))
            slot = slot_in(block_ranks(cells[:, c]), me) + k * room
            moved.append(jnp.where(down == slot, 1.0, 0.0).astype(BF16))
        place[:, q * HEAD : (q + 1) * HEAD] = lax.dot_general(
            jnp.concatenate(found, axis=1),
            jnp.concatenate(moved, axis=1),
            (((1,), (1,)), ((), ())),
            preferred_element_type=F32,
        ).astype(BF16)

    pairs = n // 2
    total_events = (nz - 1) * 2 * nh
    each = -(-(total_events - nh) // (pairs - 1))

    @pl.loop(1, pairs)
    def _(j):
        line = j % 2
        turn = j // 2
        first = 2 * lax.rem(zz // 2 + turn, npz)
        side = jnp.where(line == 0, xx, 1 - xx)

        @pl.when(line == 1)
        def _():
            for g in range(2):
                lat_cross(first + g, 1 - xx).wait_recv()

        blocks = [lat[side, first + g].astype(F32) for g in range(2)]
        embed(blocks, 0)
        base = nh + (j - 1) * each
        for e in range(each // 2):
            event(base + e)
        pair_waves(blocks)
        slot = jnp.where(line == 1, nz + first, 2 * turn)

        def put(g, i, k, v):
            put_kv(kv1, slot + g, i, k, v)

        project_kv(2, pair_cs[0], pair_cs[1], put)
        for e in range(each // 2, each):
            event(base + e)

    for j in range(1, n):
        pl.semaphore_signal(
            barrier, inc=1, device_id=(lax.rem(me + j, n), tile), device_id_type=MESH
        )

    def attend(keys_of, r, first, i):
        span = slice(first, first + n)
        last = keys_of[span, i, 2 * VID_DEV : 2 * rows].astype(F32)
        last_keys = last[:, :AUD_DEV].reshape(n * AUD_DEV, HEAD).astype(BF16)
        last_values = last[:, AUD_DEV:].reshape(n * AUD_DEV, HEAD).astype(BF16)
        keys = jnp.concatenate(
            [keys_of[span, i, 0:VID_DEV].reshape(n * VID_DEV, HEAD), last_keys], axis=0
        )
        values = jnp.concatenate(
            [keys_of[span, i, VID_DEV : 2 * VID_DEV].reshape(n * VID_DEV, HEAD), last_values],
            axis=0,
        )
        scores = lax.dot_general(
            q_ref[r, i], keys, (((1,), (1,)), ((), ())), preferred_element_type=F32
        )
        top = jnp.max(scores, axis=1, keepdims=True)
        weights = jnp.exp((scores - top) * HEAD ** (-0.5))
        total = jnp.sum(weights, axis=1, keepdims=True)
        return (dot(weights.astype(BF16), values) / total).astype(BF16)

    for step in range(STEPS):
        state = state_ref[...]
        if step > 0:

            def put_fresh(g, i, k, v):
                put_kv(kv1, n + 1, i, k, v)

            def put_mate(g, i, k, v):
                put_kv(kv1, 0, i, k, v)

            embed([state], step)
            embq[...] = padded(emb[0:rows, es])
            project_kv(1, cs_ref[0, 0], cs_ref[0, 1], put_fresh)
            project_q(1, cs_ref[0, 0], cs_ref[0, 1], (0,))
            remote(p_send, p_recv, p_ss, p_rs, mate).wait_recv()
            embed([p_recv[...].astype(F32)], step)
            project_kv(1, cs_ref[1, 0], cs_ref[1, 1], put_mate)
            project_q(1, cs_ref[1, 0], cs_ref[1, 1], (1,))
        keys_of = kv0 if step == 0 else kv1
        swaps = []
        for i in range(nh):
            if step == 0:
                for s in range(nz):
                    kv_cross(s, i, nz + s).wait_recv()
            o_send[step, i] = attend(keys_of, 1, 0, i)
            copy = remote(
                o_send.at[step, i],
                att.at[step, h, i],
                o_ss.at[step, i],
                o_rs.at[step, i],
                mate,
            )
            copy.start()
            swaps.append(copy)
        for i in range(nh):
            att[step, h, i] = attend(keys_of, 0, 2, i)
        need(5)
        for i in range(nh):
            remote(
                o_send.at[step, i],
                att.at[step, 1 - h, i],
                o_ss.at[step, i],
                o_rs.at[step, i],
                mate,
            ).wait_recv()

        heads = [att[step, a, i] for a in range(2) for i in range(nh)]
        whole = jnp.concatenate(heads, axis=1).astype(F32)
        turned = jnp.concatenate([whole[part_rows:], whole[:part_rows]], axis=0)
        mine_att = jnp.where(ty == 0, turned, whole).astype(BF16)

        def out_part(side, k):
            cs = pl.ds(pl.multiple_of(side * wing + k * chunk, HEAD), chunk)
            return dot(mine_att, w_o[:, cs])

        def tile_copy(src, dst, ss, rs, target):
            return pltpu.make_async_remote_copy(
                src_ref=src,
                dst_ref=dst,
                send_sem=ss,
                recv_sem=rs,
                device_id=(me, target),
                device_id_type=MESH,
            )

        near_rows = pl.ds(pl.multiple_of(ty * part_rows, 8), part_rows)
        first = []
        for k in range(chunks):
            s1_send[k] = out_part(1 - core, k).astype(BF16)
            copy = tile_copy(
                s1_send.at[k], s1_recv.at[k], s1_ss.at[step, k], s1_rs.at[step, k], sibling
            )
            copy.start()
            first.append(copy)
        second = []
        far_parts = []
        for k in range(chunks):
            mine = out_part(core, k)
            first[k].wait_recv()
            mine = mine + s1_recv[k].astype(F32)
            far_parts.append(mine[:part_rows])
            ks = pl.ds(k * chunk, chunk)
            acc[k] = mine[part_rows:] + embq[near_rows, ks]
            if k % 2 == 1:
                j = k // 2
                s2_send[j] = jnp.concatenate(far_parts, axis=0).astype(BF16)
                far_parts = []
                far = tile_copy(
                    s2_send.at[j], s2_recv.at[j], s2_ss.at[step, j], s2_rs.at[step, j], across
                )
                far.start()
                second.append(far)
        need(6)
        square = jnp.zeros((part_rows, 1), F32)
        part = jnp.zeros((part_rows, w_f.shape[1]), F32)
        for j, far in enumerate(second):
            far.wait_recv()
            came = s2_recv[j].astype(F32)
            for half in range(2):
                k = 2 * j + half
                mixed = acc[k] + came[half * part_rows : (half + 1) * part_rows]
                square = square + jnp.sum(mixed * mixed, axis=1, keepdims=True)
                fs = pl.ds(pl.multiple_of(core * wing + k * chunk, HEAD), chunk)
                part = part + dot((mixed * out_gain[:, fs]).astype(BF16), w_f[fs, :])
        channels = part.shape[1]
        vel_send[...] = jnp.concatenate(
            [part, jnp.broadcast_to(square, (part_rows, HEAD))], axis=1
        )
        near = tile_copy(vel_send, vel_recv, v_ss.at[step, 0], v_rs.at[step, 0], sibling)
        near.start()
        near.wait_recv()
        both = vel_send[...] + vel_recv[...]
        scale = lax.rsqrt(both[:, channels : channels + 1] / width + EPSILON)
        fresh = state_ref[near_rows, :] - step_sizes[step] * (both[:, :channels] * scale)
        st_send[...] = fresh
        over = tile_copy(st_send, st_recv.at[step], v_ss.at[step, 1], v_rs.at[step, 1], across)
        over.start()
        over.wait_recv()
        other = st_recv[step]
        new_state = jnp.concatenate(
            [jnp.where(ty == 0, fresh, other), jnp.where(ty == 0, other, fresh)], axis=0
        )
        state_ref[...] = new_state
        if step < STEPS - 1:
            p_send[...] = new_state.astype(BF16)
            remote(p_send, p_recv, p_ss, p_rs, mate).start()
        for copy in first + second + [near, over] + swaps:
            copy.wait_send()

    mine = dot(sel[...].reshape(n * sent, VID_DEV), state_ref[0:VID_DEV, :].astype(BF16))
    vid[...] = mine.astype(BF16).reshape(n, sent, HEAD)
    sends = []
    pl.semaphore_wait(barrier, n - 1)
    for j in range(1, n):
        copy = remote(
            vid.at[j], got.at[me, 0:sent], vid_ss.at[j], vid_rs.at[j], lax.rem(me + j, n)
        )
        copy.start()
        sends.append(copy)
    got[me, 0:sent] = vid[0]
    state_out[...] = state_ref[0:rows, :]

    remote(p_send, p_recv, p_ss, p_rs, mate).wait_send()
    for di in range(2):
        for d in range(1, nz):
            go, copy = lat_send(di, d)

            @pl.when(go)
            def _():
                copy.wait_send()

    for s in range(nz):
        lat_cross(s, xx).wait_send()
        for i in range(nh):
            kv_cross(s, i, 1).wait_send()

    @pl.loop(0, total_events)
    def _(e):
        for di in range(2):
            go, copy = kv_send(di, e // (2 * nh) + 1, e // nh % 2, e % nh)

            @pl.when(go)
            def _():
                copy.wait_send()

    need(7)
    for j in range(1, n):
        source = lax.rem(me - j + n, n)
        landed = got.at[source, 0:sent]
        remote(vid.at[j], landed, vid_ss.at[j], vid_rs.at[j], source).wait_recv()
    grown[...] = dot(place[...], got[...].reshape(n * room, HEAD))
    pieces = []
    for a in range(3):
        for b in range(3):
            for c in range(3):
                starts = [
                    ((h_off + b) * gw + w + c) * slots + a
                    for h_off in range(BH)
                    for w in range(bw)
                ]
                pieces.append(
                    jnp.concatenate([grown[s : s + FRAMES, :] for s in starts], axis=0).astype(BF16)
                )
    total = dot(jnp.concatenate(pieces, axis=1), w_c[...])
    conv_out[...] = total + conv_b[...]
    for copy in sends:
        copy.wait_send()


def finish(state, conv, state_out, decoded):
    state_out[...] = state[...]
    bw = decoded.shape[2]
    for h in range(BH):
        for w in range(bw):
            first = (h * bw + w) * FRAMES
            decoded[:, h, w, :] = conv[first : first + FRAMES, :].astype(BF16)


def local(
    latents,
    timestamps,
    cell_map,
    w_video,
    w_audio,
    mod_scale,
    mod_shift,
    w_query,
    w_key,
    w_value,
    q_gain,
    k_gain,
    k_cache,
    v_cache,
    w_out,
    out_gain,
    w_final,
    step_sizes,
    conv_w,
    conv_b,
):
    n, nt = lax.axis_size("patch"), lax.axis_size("tile")
    rows, channels = latents.shape
    width = w_query.shape[0]
    cols = w_query.shape[1]
    pad = -(-rows // 16) * 16
    part_rows = pad // (nt // 2)
    wing = width // 2
    chunk = 256
    chunks = wing // chunk
    nz = n // 2
    hw = cols // 2
    nh = hw // HEAD
    bw = VID_DEV // (nt * FRAMES * BH)
    border = (BH + 2) * (bw + 2) * 2 * FRAMES
    cells = FRAMES * BH * bw
    sent = -(-9 * VID_DEV // (n * nt * 16)) * 16
    room = next(r for r in (16, 32, 64, 128) if r >= sent)
    out_ch = conv_w.shape[-1]
    conv_flat = conv_w.reshape(-1, out_ch)
    vmem = pl.BlockSpec(memory_space=pltpu.VMEM)
    hbm = pl.BlockSpec(memory_space=pl.ANY)
    dma = pltpu.SemaphoreType.DMA
    state, conv = pl.pallas_call(
        functools.partial(kernel, n, nt),
        out_shape=(
            jax.ShapeDtypeStruct((rows, channels), F32),
            jax.ShapeDtypeStruct((cells, out_ch), F32),
        ),
        in_specs=[vmem] * 10 + [pl.BlockSpec(memory_space=pltpu.SMEM), vmem] + [hbm] * 8,
        out_specs=(vmem, vmem),
        scratch_shapes=[
            pltpu.VMEM(w_video.shape, BF16),
            pltpu.VMEM(w_audio.shape, BF16),
            pltpu.VMEM((width, 3 * hw), BF16),
            pltpu.VMEM(w_out.shape, BF16),
            pltpu.VMEM(w_final.shape, BF16),
            pltpu.VMEM(conv_flat.shape, BF16),
            pltpu.VMEM((n + 2 + nz, nh, 2 * rows, HEAD), BF16),
            pltpu.VMEM((n + 2, nh, 2 * rows, HEAD), BF16),
            pltpu.VMEM((2, nz, pad, HEAD), BF16),
            pltpu.VMEM((2 * rows, width), F32),
            pltpu.VMEM((2 * rows, width), BF16),
            pltpu.VMEM((pad, wing), F32),
            pltpu.VMEM((2, nh, pad, HEAD), BF16),
            pltpu.VMEM((2, 2, rows, HEAD), F32),
            pltpu.VMEM((2, 2 * rows, HEAD), F32),
            pltpu.VMEM((HEAD, 2 * HEAD), BF16),
            pltpu.VMEM((STEPS, 2, nh, pad, HEAD), BF16),
            pltpu.VMEM((STEPS, nh, pad, HEAD), BF16),
            pltpu.VMEM((pad, HEAD), BF16),
            pltpu.VMEM((pad, HEAD), BF16),
            pltpu.VMEM((pad, channels), F32),
            pltpu.VMEM((part_rows, channels), F32),
            pltpu.VMEM((STEPS, part_rows, channels), F32),
            pltpu.VMEM((chunks, part_rows, chunk), F32),
            pltpu.VMEM((chunks, pad, chunk), BF16),
            pltpu.VMEM((chunks, pad, chunk), BF16),
            pltpu.VMEM((chunks // 2, pad, chunk), BF16),
            pltpu.VMEM((chunks // 2, pad, chunk), BF16),
            pltpu.VMEM((part_rows, channels + HEAD), F32),
            pltpu.VMEM((part_rows, channels + HEAD), F32),
            pltpu.VMEM((n, sent, channels), BF16),
            pltpu.VMEM((n, room, channels), BF16),
            pltpu.VMEM((n, sent, VID_DEV), BF16),
            pltpu.VMEM((border, n * room), BF16),
            pltpu.VMEM((border, channels), F32),
            dma((8,)),
            dma((2, nz - 1)),
            dma((2, nz - 1)),
            dma((nz,)),
            dma((nz,)),
            dma((2, nz - 1, 2, nh)),
            dma((2, nz - 1, 2, nh)),
            dma((nz, nh)),
            dma((nz, nh)),
            dma((STEPS, nh)),
            dma((STEPS, nh)),
            dma(()),
            dma(()),
            dma((STEPS, chunks)),
            dma((STEPS, chunks)),
            dma((STEPS, chunks // 2)),
            dma((STEPS, chunks // 2)),
            dma((STEPS, 2)),
            dma((STEPS, 2)),
            dma((n,)),
            dma((n,)),
        ],
        compiler_params=pltpu.CompilerParams(
            collective_id=0, has_side_effects=True, vmem_limit_bytes=63 * 1024 * 1024
        ),
    )(
        latents,
        timestamps.reshape(1, -1),
        cell_map.reshape(1, -1),
        mod_scale,
        mod_shift,
        q_gain.reshape(-1, HEAD),
        k_gain.reshape(-1, HEAD),
        k_cache,
        v_cache,
        out_gain.reshape(1, -1),
        step_sizes,
        conv_b.reshape(1, -1),
        w_video,
        w_audio,
        w_query,
        w_key,
        w_value,
        w_out,
        w_final,
        conv_flat,
    )
    return pl.pallas_call(
        finish,
        out_shape=(
            jax.ShapeDtypeStruct((rows, channels), F32),
            jax.ShapeDtypeStruct((FRAMES, BH, bw, out_ch), BF16),
        ),
        in_specs=[vmem, vmem],
        out_specs=(vmem, vmem),
    )(state, conv)


def solution(mesh):
    return jax.shard_map(
        local,
        mesh=mesh,
        in_specs=(
            P("patch", None),
            P("patch"),
            P(),
            P(),
            P(),
            P(),
            P(),
            P(None, "tile"),
            P(None, "tile"),
            P(None, "tile"),
            P("tile"),
            P("tile"),
            P("patch", "tile"),
            P("patch", "tile"),
            P("tile", None),
            P(),
            P(),
            P(),
            P(),
            P(),
        ),
        out_specs=(P("patch", None), P(None, "patch", "tile", None)),
        check_vma=False,
    )
```

```python
import functools
import math

import jax
import jax.numpy as jnp
from jax import lax
from jax.experimental import pallas as pl
from jax.experimental.pallas import tpu as pltpu
from jax.sharding import PartitionSpec as P

HEAD = 128
VID_DEV = 128
AUD_DEV = 8
STEPS = 2
FRAMES = 8
BH = 2
EPSILON = 1e-06
SCALE = HEAD ** (-0.5) * math.log2(math.e)
MESH = pl.DeviceIdType.MESH
F32 = jnp.float32
BF16 = jnp.bfloat16


def dot(a, b):
    return jnp.dot(a, b, preferred_element_type=F32)


def kernel(
    n,
    nt,
    latents,
    stamps,
    cells,
    mod_scale,
    mod_shift,
    q_gain,
    k_gain,
    k_cache,
    v_cache,
    out_gain,
    step_sizes,
    conv_b,
    wv_hbm,
    wa_hbm,
    wq_hbm,
    wk_hbm,
    wval_hbm,
    wo_hbm,
    wf_hbm,
    cw_hbm,
    state_out,
    conv_out,
    w_vid,
    w_aud,
    w_qkv,
    w_o,
    w_f,
    kv0,
    kv1,
    lat,
    emb,
    normed,
    q_ref,
    cs_ref,
    pair_cs,
    table,
    att,
    o_send,
    state_ref,
    st_send,
    st_recv,
    acc,
    s1_send,
    s1_recv,
    s2_send,
    s2_recv,
    vel_send,
    vel_recv,
    vid,
    got,
    sel,
    place,
    grown,
    load_sem,
    lz_ss,
    lz_rs,
    lx_ss,
    lx_rs,
    kz_ss,
    kz_rs,
    kx_ss,
    kx_rs,
    o_ss,
    o_rs,
    s1_ss,
    s1_rs,
    s2_ss,
    s2_rs,
    v_ss,
    v_rs,
    vid_ss,
    vid_rs,
):
    rows = latents.shape[0]
    pad = lat.shape[2]
    width = emb.shape[1]
    hw = w_qkv.shape[1] // 6
    nh = hw // HEAD
    part_rows = pad // (nt // 2)
    wing = width // 2
    taps, out_ch = cw_hbm.shape
    nz = n // 2
    npz = nz // 2
    me = lax.axis_index("patch")
    tile = lax.axis_index("tile")
    core = tile % 2
    ty = tile // 2
    chunks = acc.shape[0]
    chunk = acc.shape[2]
    zz = me // 2
    xx = me % 2
    h = zz % 2
    mate = me + 2 - 4 * h

    def half_cols(a):
        return pl.ds(pl.multiple_of(a * hw, HEAD), hw)

    loads = []
    for i, (src, dst) in enumerate(
        (
            (wv_hbm, w_vid),
            (wa_hbm, w_aud),
            (wk_hbm.at[:, half_cols(h)], w_qkv.at[:, 0:hw]),
            (wval_hbm.at[:, half_cols(h)], w_qkv.at[:, hw : 2 * hw]),
            (wq_hbm.at[:, half_cols(h)], w_qkv.at[:, 2 * hw : 3 * hw]),
            (wo_hbm, w_o),
            (wf_hbm, w_f),
            (cw_hbm.at[0:width], w_qkv.at[:, 0:out_ch]),
            (cw_hbm.at[width:taps], w_qkv.at[0 : taps - width, out_ch : 2 * out_ch]),
            (wk_hbm.at[:, half_cols(1 - h)], w_qkv.at[:, 3 * hw : 4 * hw]),
            (wval_hbm.at[:, half_cols(1 - h)], w_qkv.at[:, 4 * hw : 5 * hw]),
            (wq_hbm.at[:, half_cols(1 - h)], w_qkv.at[:, 5 * hw : 6 * hw]),
        )
    ):
        loads.append(pltpu.make_async_copy(src, dst, load_sem.at[i]))
    for i in (0, 1, 2, 3, 4, 9, 10, 11, 5, 6):
        loads[i].start()

    got[...] = jnp.zeros(got.shape, BF16)
    barrier = pltpu.get_barrier_semaphore()
    for z, z_there in ((-1, zz > 0), (1, zz < nz - 1)):

        @pl.when(z_there)
        def _():
            pl.semaphore_signal(
                barrier, inc=1, device_id=(me + 2 * z, tile), device_id_type=MESH
            )

    sibling = ty * 2 + 1 - core
    across = (1 - ty) * 2 + core
    for spot in ((me + 1 - 2 * xx, tile), (me, sibling), (me, across)):
        pl.semaphore_signal(barrier, inc=1, device_id=spot, device_id_type=MESH)

    def padded(x):
        return jnp.concatenate([x, jnp.zeros((pad - rows, x.shape[1]), F32)], axis=0)

    line_row = lax.broadcasted_iota(jnp.int32, (pad - rows, HEAD), 0)
    aud_stamps = jnp.concatenate(
        [stamps[:, VID_DEV:rows], jnp.zeros((1, HEAD - AUD_DEV), jnp.int32)], axis=1
    ).astype(F32)
    vid_stamps = stamps[:, 0:VID_DEV].astype(F32)
    tail = jnp.where(line_row == 0, vid_stamps, jnp.where(line_row == 1, aud_stamps, 0.0))
    lat[xx, zz] = jnp.concatenate([latents[...], tail], axis=0).astype(BF16)

    def put_kv(where, slot, i, k, v):
        where[slot, i, 0:VID_DEV] = k[:VID_DEV].astype(BF16)
        where[slot, i, VID_DEV : 2 * VID_DEV] = v[:VID_DEV].astype(BF16)
        last = jnp.concatenate([k[VID_DEV:], v[VID_DEV:]], axis=0)
        where[slot, i, 2 * VID_DEV : 2 * rows] = last.astype(BF16)

    for i in range(nh):
        for a, slot in ((h, 1), (1 - h, n + 2 + zz)):
            cs = pl.ds(pl.multiple_of(a * hw + i * HEAD, HEAD), HEAD)
            put_kv(kv0, slot, i, k_cache[:, cs].astype(F32), v_cache[:, cs].astype(F32))
    pl.semaphore_wait(barrier, 5 - jnp.where((zz == 0) | (zz == nz - 1), 1, 0))

    def remote(src, dst, ss, rs, patch):
        return pltpu.make_async_remote_copy(
            src_ref=src,
            dst_ref=dst,
            send_sem=ss,
            recv_sem=rs,
            device_id=(patch, tile),
            device_id_type=MESH,
        )

    def inside_line(z):
        return (z >= 0) & (z < nz)

    def lat_send(di, d):
        step = 1 - 2 * di
        s = zz - step * (d - 1)
        copy = remote(
            lat.at[xx, s], lat.at[xx, s], lz_ss.at[di, d - 1], lz_rs.at[di, d - 1], me + 2 * step
        )
        return inside_line(s) & inside_line(zz + step), copy

    def lat_arrive(di, d):
        step = 1 - 2 * di
        s = zz - step * d
        copy = remote(
            lat.at[xx, s], lat.at[xx, s], lz_ss.at[di, d - 1], lz_rs.at[di, d - 1], me - 2 * step
        )
        return inside_line(s), s, copy

    def lat_cross(s, line):
        return remote(
            lat.at[line, s], lat.at[line, s], lx_ss.at[s], lx_rs.at[s], me + 1 - 2 * xx
        )

    def lat_event(d):
        for di in range(2):
            there, s, copy = lat_arrive(di, d)

            @pl.when(there)
            def _():
                copy.wait_recv()
                if d + 1 < nz:
                    onward, forward = lat_send(di, d + 1)

                    @pl.when(onward)
                    def _():
                        forward.start()

                lat_cross(s, xx).start()

    def slot_of(z, s, a):
        other = 2 * lax.rem(s // 2 - z // 2 + npz, npz) + s % 2
        slot = jnp.where(s == z, 1, jnp.where(s == z + 1 - 2 * (z % 2), n, other))
        return jnp.where(a == z % 2, slot, n + 2 + s)

    def half_of(di, kind):
        return (1 - di) + kind * (2 * di - 1)

    def wanted_at(di, kind, z):
        return (kind == 0) | (z != (nz - 1 if di == 0 else 0))

    def kv_send(di, d, kind, i):
        step = 1 - 2 * di
        s = zz - step * (d - 1)
        a = half_of(di, kind)
        copy = remote(
            kv0.at[slot_of(zz, s, a), i],
            kv0.at[slot_of(zz + step, s, a), i],
            kz_ss.at[di, d - 1, kind, i],
            kz_rs.at[di, d - 1, kind, i],
            me + 2 * step,
        )
        return inside_line(s) & inside_line(zz + step) & wanted_at(di, kind, zz + step), copy

    def kv_cross(s, i, slot):
        return remote(
            kv0.at[slot, i], kv0.at[nz + s, i], kx_ss.at[s, i], kx_rs.at[s, i], me + 1 - 2 * xx
        )

    def event(e):
        d = e // (2 * nh) + 1
        kind = e // nh % 2
        i = e % nh
        for di in range(2):
            step = 1 - 2 * di
            s = zz - step * d
            a = half_of(di, kind)
            slot = slot_of(zz, s, a)

            @pl.when(inside_line(s) & wanted_at(di, kind, zz))
            def _():
                remote(
                    kv0.at[slot, i],
                    kv0.at[slot, i],
                    kz_ss.at[di, d - 1, kind, i],
                    kz_rs.at[di, d - 1, kind, i],
                    me - 2 * step,
                ).wait_recv()
                onward, forward = kv_send(di, d + 1, kind, i)

                @pl.when(onward)
                def _():
                    forward.start()

                @pl.when(a == h)
                def _():
                    kv_cross(s, i, slot).start()

    def start_own(kind, pieces):
        for i in pieces:
            for di in range(2):
                go, copy = kv_send(di, 1, kind, i)

                @pl.when(go)
                def _():
                    copy.start()

    for di in range(2):
        go, copy = lat_send(di, 1)

        @pl.when(go)
        def _():
            copy.start()

    lat_cross(zz, xx).start()
    start_own(0, (0,))
    kv_cross(zz, 0, 1).start()

    lane = lax.broadcasted_iota(jnp.int32, (1, HEAD), 1)
    frequency = jnp.exp(-jnp.log(F32(10000.0)) * (lane % (HEAD // 2)).astype(F32) / (HEAD // 2))
    times = lax.broadcasted_iota(jnp.int32, (HEAD // 2, HEAD), 0).astype(F32)
    angles = times * frequency
    waves = (jnp.cos(angles), jnp.where(lane < HEAD // 2, -1.0, 1.0) * jnp.sin(angles))
    for k, wave in enumerate(waves):
        top = wave.astype(BF16)
        cs = slice(k * HEAD, (k + 1) * HEAD)
        table[0 : HEAD // 2, cs] = top
        table[HEAD // 2 : HEAD, cs] = (wave - top.astype(F32)).astype(BF16)

    waited = set()

    def need(i):
        if i not in waited:
            loads[i].wait()
            waited.add(i)

    def embed(blocks, step):
        count = len(blocks)
        size = count * rows
        vid_b = jnp.concatenate([b[:VID_DEV] for b in blocks], axis=0).astype(BF16)
        aud_b = jnp.concatenate([b[VID_DEV:rows] for b in blocks], axis=0).astype(BF16)
        square = jnp.zeros((size, 1), F32)
        wide = width // 4
        for i in range(4):
            c = slice(i * wide, (i + 1) * wide)
            e = jnp.concatenate([dot(vid_b, w_vid[:, c]), dot(aud_b, w_aud[:, c])], axis=0)
            emb[0:size, c] = e
            square = square + jnp.sum(e * e, axis=1, keepdims=True)
        scale = lax.rsqrt(square / width + EPSILON)
        for i in range(4):
            c = slice(i * wide, (i + 1) * wide)
            x = emb[0:size, c] * scale * (1.0 + mod_scale[step : step + 1, c])
            normed[0:size, c] = (x + mod_shift[step : step + 1, c]).astype(BF16)

    def shard_rows(x, g, count):
        if count == 1:
            return x
        first = count * VID_DEV + g * AUD_DEV
        return jnp.concatenate(
            [x[g * VID_DEV : (g + 1) * VID_DEV], x[first : first + AUD_DEV]], axis=0
        )

    def rotate(x, gain, cos, sin):
        x = x * lax.rsqrt(jnp.mean(x * x, axis=1, keepdims=True) + EPSILON)
        x = x * gain
        return x * cos + pltpu.roll(x, HEAD // 2, 1) * sin

    def gain_row(gain, a, i):
        return gain[pl.ds((h if a == 0 else 1 - h) * nh + i, 1), :]

    def project_kv(count, a, cos, sin, put):
        raw = dot(normed[0 : count * rows, :], w_qkv[:, 3 * a * hw : (3 * a + 2) * hw])
        for i in range(nh):
            k = rotate(raw[:, i * HEAD : (i + 1) * HEAD], gain_row(k_gain, a, i), cos, sin)
            v = raw[:, hw + i * HEAD : hw + (i + 1) * HEAD]
            for g in range(count):
                put(g, a, i, shard_rows(k, g, count), shard_rows(v, g, count))

    def project_q(count, a, cos, sin, targets):
        raw = dot(normed[0 : count * rows, :], w_qkv[:, (3 * a + 2) * hw : 3 * (a + 1) * hw])
        for i in range(nh):
            gain = gain_row(q_gain, a, i) * SCALE
            q = rotate(raw[:, i * HEAD : (i + 1) * HEAD], gain, cos, sin)
            for g in range(count):
                q_ref[targets[g], i] = padded(shard_rows(q, g, count)).astype(BF16)

    spot = lax.broadcasted_iota(jnp.int32, (HEAD, 3 * HEAD), 0) % (HEAD // 2)

    def pair_waves(blocks):
        aud = jnp.where(
            lane < AUD_DEV,
            blocks[0][rows + 1 : rows + 2],
            pltpu.roll(blocks[1][rows + 1 : rows + 2], AUD_DEV, 1),
        )
        line = jnp.concatenate([b[rows : rows + 1] for b in blocks] + [aud], axis=1)
        chosen = jnp.where(spot == line.astype(jnp.int32), 1.0, 0.0).astype(BF16)
        both = lax.dot_general(
            chosen, table[...], (((0,), (0,)), ((), ())), preferred_element_type=F32
        )
        pair_cs[0] = both[0 : 2 * rows, 0:HEAD]
        pair_cs[1] = both[0 : 2 * rows, HEAD : 2 * HEAD]

    state_ref[...] = padded(latents[...])

    lat_event(1)
    start_own(0, range(1, nh))
    for i in range(1, nh):
        kv_cross(zz, i, 1).start()

    own_blocks = [lat[xx, zz].astype(F32), lat[xx, zz + 1 - 2 * h].astype(F32)]
    need(0)
    need(1)
    embed(own_blocks, 0)

    def keep_near(count):
        for k in range(chunks):
            es = pl.ds(pl.multiple_of(core * wing + k * chunk, HEAD), chunk)
            last = emb[count * VID_DEV : count * VID_DEV + AUD_DEV, es]
            full = padded(jnp.concatenate([emb[0:VID_DEV, es], last], axis=0))
            acc[k] = jnp.where(ty == 0, full[:part_rows], full[part_rows:])

    keep_near(2)
    if nz > 2:
        lat_event(2)
    start_own(1, range(nh))
    pair_waves(own_blocks)
    for k in range(2):
        cs_ref[k] = shard_rows(pair_cs[k], 0, 2)

    def put_own(g, a, i, k, v):
        if a == 0:
            put_kv(kv0, n + 1 if g == 0 else 0, i, k, v)
        if g == 1:
            put_kv(kv1.at[a], 0, i, k, v)

    need(2)
    need(3)
    project_kv(2, 0, pair_cs[0], pair_cs[1], put_own)
    for d in range(3, nz):
        lat_event(d)
    need(4)
    project_q(2, 0, pair_cs[0], pair_cs[1], (0, 1))
    for e in range(nh):
        event(e)
    need(9)
    need(10)
    project_kv(2, 1, pair_cs[0], pair_cs[1], put_own)
    for e in range(nh, 2 * nh):
        event(e)

    bw = VID_DEV // (nt * FRAMES * BH)
    gw = bw + 2
    slots = 2 * FRAMES
    high, wide_w = n * BH, nt * bw
    share = VID_DEV // (n * nt)
    sent = sel.shape[1]
    room = got.shape[1]
    group = HEAD // room
    row = lax.broadcasted_iota(jnp.int32, (place.shape[0], 1), 0)
    f_id = row % slots - 1
    h_id = row // (slots * gw) - 1 + me * BH
    w_id = row // slots % gw - 1 + tile * bw
    inside = (
        (f_id >= 0)
        & (f_id < FRAMES)
        & (h_id >= 0)
        & (h_id < high)
        & (w_id >= 0)
        & (w_id < wide_w)
    )
    wanted = jnp.where(inside, (f_id * high + h_id) * wide_w + w_id, -1)
    down = lax.broadcasted_iota(jnp.int32, (VID_DEV, VID_DEV), 0)
    along = lax.broadcasted_iota(jnp.int32, (VID_DEV, VID_DEV), 1)

    def block_ranks(cell):
        bh = cell // wide_w % high // BH
        bc = cell % wide_w // bw
        block = (bh * nt + bc).astype(F32)
        column = jnp.sum(jnp.where(down == along, block, 0.0), axis=1, keepdims=True)
        ahead = jnp.where((column == block) & (down < along), 1.0, 0.0)
        return bh, bc, jnp.sum(ahead, axis=0, keepdims=True).astype(jnp.int32)

    def slot_in(ranks, p):
        bh, bc, rank = ranks
        dh = bh - p + 1
        dw = bc - tile + 1
        near_by = (dh >= 0) & (dh < 3) & (dw >= 0) & (dw < 3)
        return jnp.where(near_by, (dh * 3 + dw) * share + rank, -HEAD)

    my_ranks = block_ranks(cells[:, pl.ds(pl.multiple_of(me * VID_DEV, VID_DEV), VID_DEV)])
    pick = lax.broadcasted_iota(jnp.int32, (sent, VID_DEV), 0)
    for j in range(n):
        slot = slot_in(my_ranks, lax.rem(me + j, n))
        sel[j] = jnp.where(pick == slot, 1.0, 0.0).astype(BF16)
    for q in range(n // group):
        found, moved = [], []
        for k in range(group):
            c = slice((q * group + k) * VID_DEV, (q * group + k + 1) * VID_DEV)
            found.append(jnp.where(cells[:, c] == wanted, 1.0, 0.0).astype(BF16))
            slot = slot_in(block_ranks(cells[:, c]), me) + k * room
            moved.append(jnp.where(down == slot, 1.0, 0.0).astype(BF16))
        place[:, q * HEAD : (q + 1) * HEAD] = lax.dot_general(
            jnp.concatenate(found, axis=1),
            jnp.concatenate(moved, axis=1),
            (((1,), (1,)), ((), ())),
            preferred_element_type=F32,
        ).astype(BF16)

    pairs = n // 2
    total_events = (nz - 1) * 2 * nh
    each = -(-(total_events - 2 * nh) // (pairs - 1))
    marks = [each * k // 3 for k in range(4)]

    early = pairs // 4

    def pair_of(j):
        line = j % 2
        turn = j // 2
        first = 2 * lax.rem(zz // 2 + turn, npz)
        side = jnp.where(line == 0, xx, 1 - xx)
        return line, first, side, jnp.where(line == 1, nz + first, 2 * turn)

    def put_at(slot):
        def put(g, a, i, k, v):
            put_kv(kv1.at[a], slot + g, i, k, v)

        return put

    @pl.loop(1, pairs)
    def _(j):
        line, first, side, slot = pair_of(j)

        @pl.when(line == 1)
        def _():
            for g in range(2):
                lat_cross(first + g, 1 - xx).wait_recv()

        blocks = [lat[side, first + g].astype(F32) for g in range(2)]
        embed(blocks, 0)
        base = 2 * nh + (j - 1) * each
        for e in range(marks[0], marks[1]):
            event(base + e)
        pair_waves(blocks)
        project_kv(2, 0, pair_cs[0], pair_cs[1], put_at(slot))
        for e in range(marks[1], marks[2]):
            event(base + e)

        @pl.when(j <= early)
        def _():
            project_kv(2, 1, pair_cs[0], pair_cs[1], put_at(slot))

        for e in range(marks[2], marks[3]):
            event(base + e)

    def late_pairs():
        @pl.loop(early + 1, pairs)
        def _(j):
            line, first, side, slot = pair_of(j)
            blocks = [lat[side, first + g].astype(F32) for g in range(2)]
            embed(blocks, 0)
            pair_waves(blocks)
            project_kv(2, 1, pair_cs[0], pair_cs[1], put_at(slot))

    for j in range(1, n):
        pl.semaphore_signal(
            barrier, inc=1, device_id=(lax.rem(me + j, n), tile), device_id_type=MESH
        )

    def score(keys_of, r, first, i):
        span = slice(first, first + n)
        last = keys_of[span, i, 2 * VID_DEV : 2 * rows].astype(F32)
        last_keys = last[:, :AUD_DEV].reshape(n * AUD_DEV, HEAD).astype(BF16)
        last_values = last[:, AUD_DEV:].reshape(n * AUD_DEV, HEAD).astype(BF16)
        keys = jnp.concatenate(
            [keys_of[span, i, 0:VID_DEV].reshape(n * VID_DEV, HEAD), last_keys], axis=0
        )
        values = jnp.concatenate(
            [keys_of[span, i, VID_DEV : 2 * VID_DEV].reshape(n * VID_DEV, HEAD), last_values],
            axis=0,
        )
        scores = lax.dot_general(
            q_ref[r, i], keys, (((1,), (1,)), ((), ())), preferred_element_type=F32
        )
        return scores, jnp.max(scores, axis=1, keepdims=True), values

    def attend(held):
        scores, top, values = held
        weights = jnp.exp2(scores - top)
        total = jnp.sum(weights, axis=1, keepdims=True)
        return (dot(weights.astype(BF16), values) / total).astype(BF16)

    batch = nh if n * rows <= 2048 else 1

    def attend_all(keys_of, r, first, result):
        for k in range(0, nh, batch):
            held = [score(keys_of, r, first, i) for i in range(k, min(k + batch, nh))]
            for i, parts in enumerate(held):
                result[k + i] = attend(parts)

    for step in range(STEPS):
        state = state_ref[...]
        if step == 0:
            swaps = []
            for i in range(nh):
                for s in range(nz):
                    kv_cross(s, i, nz + s).wait_recv()
                o_send[i] = attend(score(kv0, 1, 0, i))
                copy = remote(o_send.at[i], att.at[h, i], o_ss.at[i], o_rs.at[i], mate)
                copy.start()
                swaps.append(copy)
            attend_all(kv0, 0, 2, att.at[h])
            need(5)
            for i in range(nh):
                remote(
                    o_send.at[i], att.at[1 - h, i], o_ss.at[i], o_rs.at[i], mate
                ).wait_recv()
        else:

            def put_fresh(g, a, i, k, v):
                put_kv(kv1.at[a], 1, i, k, v)

            embed([state], step)
            keep_near(1)
            need(11)
            for a in range(2):
                project_kv(1, a, cs_ref[0], cs_ref[1], put_fresh)
                project_q(1, a, cs_ref[0], cs_ref[1], (a,))
            for i in (7, 8):
                loads[i].start()
            for a in range(2):
                attend_all(kv1.at[a], a, 0, att.at[h if a == 0 else 1 - h])

        heads = [att[a, i] for a in range(2) for i in range(nh)]
        whole = jnp.concatenate(heads, axis=1).astype(F32)
        turned = jnp.concatenate([whole[part_rows:], whole[:part_rows]], axis=0)
        mine_att = jnp.where(ty == 0, turned, whole).astype(BF16)

        def out_part(side, k):
            cs = pl.ds(pl.multiple_of(side * wing + k * chunk, HEAD), chunk)
            return dot(mine_att, w_o[:, cs])

        def tile_copy(src, dst, ss, rs, target):
            return pltpu.make_async_remote_copy(
                src_ref=src,
                dst_ref=dst,
                send_sem=ss,
                recv_sem=rs,
                device_id=(me, target),
                device_id_type=MESH,
            )

        near_rows = pl.ds(pl.multiple_of(ty * part_rows, 8), part_rows)
        first = []
        for k in range(chunks):
            s1_send[k] = out_part(1 - core, k).astype(BF16)
            copy = tile_copy(
                s1_send.at[k], s1_recv.at[k], s1_ss.at[step, k], s1_rs.at[step, k], sibling
            )
            copy.start()
            first.append(copy)
        second = []
        far_parts = []
        for k in range(chunks):
            mine = out_part(core, k)
            first[k].wait_recv()
            mine = mine + s1_recv[k].astype(F32)
            far_parts.append(mine[:part_rows])
            acc[k] += mine[part_rows:]
            if k % 2 == 1:
                j = k // 2
                s2_send[j] = jnp.concatenate(far_parts, axis=0).astype(BF16)
                far_parts = []
                far = tile_copy(
                    s2_send.at[j], s2_recv.at[j], s2_ss.at[step, j], s2_rs.at[step, j], across
                )
                far.start()
                second.append(far)
        if step == 0:
            late_pairs()
        need(6)
        square = jnp.zeros((part_rows, 1), F32)
        part = jnp.zeros((part_rows, w_f.shape[1]), F32)
        for j, far in enumerate(second):
            far.wait_recv()
            came = s2_recv[j].astype(F32)
            for half in range(2):
                k = 2 * j + half
                mixed = acc[k] + came[half * part_rows : (half + 1) * part_rows]
                square = square + jnp.sum(mixed * mixed, axis=1, keepdims=True)
                fs = pl.ds(pl.multiple_of(core * wing + k * chunk, HEAD), chunk)
                part = part + dot((mixed * out_gain[:, fs]).astype(BF16), w_f[fs, :])
        channels = part.shape[1]
        vel_send[...] = jnp.concatenate(
            [part, jnp.broadcast_to(square, (part_rows, HEAD))], axis=1
        )
        near = tile_copy(vel_send, vel_recv, v_ss.at[step, 0], v_rs.at[step, 0], sibling)
        near.start()
        near.wait_recv()
        both = vel_send[...] + vel_recv[...]
        scale = lax.rsqrt(both[:, channels : channels + 1] / width + EPSILON)
        fresh = state_ref[near_rows, :] - step_sizes[step] * (both[:, :channels] * scale)
        st_send[...] = fresh
        over = tile_copy(st_send, st_recv.at[step], v_ss.at[step, 1], v_rs.at[step, 1], across)
        over.start()
        over.wait_recv()
        other = st_recv[step]
        new_state = jnp.concatenate(
            [jnp.where(ty == 0, fresh, other), jnp.where(ty == 0, other, fresh)], axis=0
        )
        state_ref[...] = new_state
        for copy in first + second + [near, over] + (swaps if step == 0 else []):
            copy.wait_send()

    mine = dot(sel[...].reshape(n * sent, VID_DEV), state_ref[0:VID_DEV, :].astype(BF16))
    vid[...] = mine.astype(BF16).reshape(n, sent, HEAD)
    sends = []
    pl.semaphore_wait(barrier, n - 1)
    for j in range(1, n):
        copy = remote(
            vid.at[j], got.at[me, 0:sent], vid_ss.at[j], vid_rs.at[j], lax.rem(me + j, n)
        )
        copy.start()
        sends.append(copy)
    got[me, 0:sent] = vid[0]
    state_out[...] = state_ref[0:rows, :]

    for di in range(2):
        for d in range(1, nz):
            go, copy = lat_send(di, d)

            @pl.when(go)
            def _():
                copy.wait_send()

    for s in range(nz):
        lat_cross(s, xx).wait_send()
        for i in range(nh):
            kv_cross(s, i, 1).wait_send()

    @pl.loop(0, total_events)
    def _(e):
        for di in range(2):
            go, copy = kv_send(di, e // (2 * nh) + 1, e // nh % 2, e % nh)

            @pl.when(go)
            def _():
                copy.wait_send()

    need(7)
    need(8)
    for j in range(1, n):
        source = lax.rem(me - j + n, n)
        landed = got.at[source, 0:sent]
        remote(vid.at[j], landed, vid_ss.at[j], vid_rs.at[j], source).wait_recv()
    grown[...] = dot(place[...], got[...].reshape(n * room, HEAD))
    pieces = []
    for a in range(3):
        for b in range(3):
            for c in range(3):
                starts = [
                    ((h_off + b) * gw + w + c) * slots + a
                    for h_off in range(BH)
                    for w in range(bw)
                ]
                pieces.append(
                    jnp.concatenate([grown[s : s + FRAMES, :] for s in starts], axis=0).astype(BF16)
                )
    cut = width // HEAD
    total = dot(jnp.concatenate(pieces[:cut], axis=1), w_qkv[:, 0:out_ch])
    rest = w_qkv[0 : taps - width, out_ch : 2 * out_ch]
    total = total + dot(jnp.concatenate(pieces[cut:], axis=1), rest)
    conv_out[...] = total + conv_b[...]
    for copy in sends:
        copy.wait_send()


def finish(state, conv, state_out, decoded):
    state_out[...] = state[...]
    bw = decoded.shape[2]
    for h in range(BH):
        for w in range(bw):
            first = (h * bw + w) * FRAMES
            decoded[:, h, w, :] = conv[first : first + FRAMES, :].astype(BF16)


def local(
    latents,
    timestamps,
    cell_map,
    w_video,
    w_audio,
    mod_scale,
    mod_shift,
    w_query,
    w_key,
    w_value,
    q_gain,
    k_gain,
    k_cache,
    v_cache,
    w_out,
    out_gain,
    w_final,
    step_sizes,
    conv_w,
    conv_b,
):
    n, nt = lax.axis_size("patch"), lax.axis_size("tile")
    rows, channels = latents.shape
    width = w_query.shape[0]
    cols = w_query.shape[1]
    pad = -(-rows // 16) * 16
    part_rows = pad // (nt // 2)
    wing = width // 2
    chunk = 256
    chunks = wing // chunk
    nz = n // 2
    hw = cols // 2
    nh = hw // HEAD
    bw = VID_DEV // (nt * FRAMES * BH)
    border = (BH + 2) * (bw + 2) * 2 * FRAMES
    cells = FRAMES * BH * bw
    sent = -(-9 * VID_DEV // (n * nt * 16)) * 16
    room = next(r for r in (16, 32, 64, 128) if r >= sent)
    out_ch = conv_w.shape[-1]
    conv_flat = conv_w.reshape(-1, out_ch)
    vmem = pl.BlockSpec(memory_space=pltpu.VMEM)
    hbm = pl.BlockSpec(memory_space=pl.ANY)
    dma = pltpu.SemaphoreType.DMA
    state, conv = pl.pallas_call(
        functools.partial(kernel, n, nt),
        out_shape=(
            jax.ShapeDtypeStruct((rows, channels), F32),
            jax.ShapeDtypeStruct((cells, out_ch), F32),
        ),
        in_specs=[vmem] * 10 + [pl.BlockSpec(memory_space=pltpu.SMEM), vmem] + [hbm] * 8,
        out_specs=(vmem, vmem),
        scratch_shapes=[
            pltpu.VMEM(w_video.shape, BF16),
            pltpu.VMEM(w_audio.shape, BF16),
            pltpu.VMEM((width, 6 * hw), BF16),
            pltpu.VMEM(w_out.shape, BF16),
            pltpu.VMEM(w_final.shape, BF16),
            pltpu.VMEM((n + 2 + nz, nh, 2 * rows, HEAD), BF16),
            pltpu.VMEM((2, n, nh, 2 * rows, HEAD), BF16),
            pltpu.VMEM((2, nz, pad, HEAD), BF16),
            pltpu.VMEM((2 * rows, width), F32),
            pltpu.VMEM((2 * rows, width), BF16),
            pltpu.VMEM((2, nh, pad, HEAD), BF16),
            pltpu.VMEM((2, rows, HEAD), F32),
            pltpu.VMEM((2, 2 * rows, HEAD), F32),
            pltpu.VMEM((HEAD, 2 * HEAD), BF16),
            pltpu.VMEM((2, nh, pad, HEAD), BF16),
            pltpu.VMEM((nh, pad, HEAD), BF16),
            pltpu.VMEM((pad, channels), F32),
            pltpu.VMEM((part_rows, channels), F32),
            pltpu.VMEM((STEPS, part_rows, channels), F32),
            pltpu.VMEM((chunks, part_rows, chunk), F32),
            pltpu.VMEM((chunks, pad, chunk), BF16),
            pltpu.VMEM((chunks, pad, chunk), BF16),
            pltpu.VMEM((chunks // 2, pad, chunk), BF16),
            pltpu.VMEM((chunks // 2, pad, chunk), BF16),
            pltpu.VMEM((part_rows, channels + HEAD), F32),
            pltpu.VMEM((part_rows, channels + HEAD), F32),
            pltpu.VMEM((n, sent, channels), BF16),
            pltpu.VMEM((n, room, channels), BF16),
            pltpu.VMEM((n, sent, VID_DEV), BF16),
            pltpu.VMEM((border, n * room), BF16),
            pltpu.VMEM((border, channels), F32),
            dma((12,)),
            dma((2, nz - 1)),
            dma((2, nz - 1)),
            dma((nz,)),
            dma((nz,)),
            dma((2, nz - 1, 2, nh)),
            dma((2, nz - 1, 2, nh)),
            dma((nz, nh)),
            dma((nz, nh)),
            dma((nh,)),
            dma((nh,)),
            dma((STEPS, chunks)),
            dma((STEPS, chunks)),
            dma((STEPS, chunks // 2)),
            dma((STEPS, chunks // 2)),
            dma((STEPS, 2)),
            dma((STEPS, 2)),
            dma((n,)),
            dma((n,)),
        ],
        compiler_params=pltpu.CompilerParams(
            collective_id=0, has_side_effects=True, vmem_limit_bytes=63 * 1024 * 1024
        ),
    )(
        latents,
        timestamps.reshape(1, -1),
        cell_map.reshape(1, -1),
        mod_scale,
        mod_shift,
        q_gain.reshape(-1, HEAD),
        k_gain.reshape(-1, HEAD),
        k_cache,
        v_cache,
        out_gain.reshape(1, -1),
        step_sizes,
        conv_b.reshape(1, -1),
        w_video,
        w_audio,
        w_query,
        w_key,
        w_value,
        w_out,
        w_final,
        conv_flat,
    )
    return pl.pallas_call(
        finish,
        out_shape=(
            jax.ShapeDtypeStruct((rows, channels), F32),
            jax.ShapeDtypeStruct((FRAMES, BH, bw, out_ch), BF16),
        ),
        in_specs=[vmem, vmem],
        out_specs=(vmem, vmem),
    )(state, conv)


def solution(mesh):
    return jax.shard_map(
        local,
        mesh=mesh,
        in_specs=(
            P("patch", None),
            P("patch"),
            P(),
            P(),
            P(),
            P(),
            P(),
            P(None, "tile"),
            P(None, "tile"),
            P(None, "tile"),
            P("tile"),
            P("tile"),
            P("patch", "tile"),
            P("patch", "tile"),
            P("tile", None),
            P(),
            P(),
            P(),
            P(),
            P(),
        ),
        out_specs=(P("patch", None), P(None, "patch", "tile", None)),
        check_vma=False,
    )
```

```python
import functools
import math

import jax
import jax.numpy as jnp
from jax import lax
from jax.experimental import pallas as pl
from jax.experimental.pallas import tpu as pltpu
from jax.sharding import PartitionSpec as P

HEAD = 128
VID_DEV = 128
AUD_DEV = 8
STEPS = 2
FRAMES = 8
BH = 2
EPSILON = 1e-06
SCALE = HEAD ** (-0.5) * math.log2(math.e)
MESH = pl.DeviceIdType.MESH
F32 = jnp.float32
BF16 = jnp.bfloat16


def dot(a, b):
    return jnp.dot(a, b, preferred_element_type=F32)


def kernel(
    n,
    nt,
    latents,
    stamps,
    cells,
    mod_scale,
    mod_shift,
    q_gain,
    k_gain,
    k_cache,
    v_cache,
    out_gain,
    step_sizes,
    conv_b,
    wv_hbm,
    wa_hbm,
    wq_hbm,
    wk_hbm,
    wval_hbm,
    wo_hbm,
    wf_hbm,
    cw_hbm,
    state_out,
    conv_out,
    w_vid,
    w_aud,
    w_qkv,
    w_o,
    w_f,
    kv0,
    kv1,
    lat,
    emb,
    normed,
    q_ref,
    cs_ref,
    pair_cs,
    table,
    att,
    o_send,
    state_ref,
    st_send,
    st_recv,
    acc,
    s1_send,
    s1_recv,
    s2_send,
    s2_recv,
    vel_send,
    vel_recv,
    vid,
    got,
    sel,
    place,
    grown,
    load_sem,
    lz_ss,
    lz_rs,
    lx_ss,
    lx_rs,
    kz_ss,
    kz_rs,
    kx_ss,
    kx_rs,
    o_ss,
    o_rs,
    s1_ss,
    s1_rs,
    s2_ss,
    s2_rs,
    v_ss,
    v_rs,
    vid_ss,
    vid_rs,
):
    rows = latents.shape[0]
    pad = lat.shape[2]
    width = emb.shape[1]
    hw = w_qkv.shape[1] // 6
    nh = hw // HEAD
    part_rows = pad // (nt // 2)
    wing = width // 2
    taps, out_ch = cw_hbm.shape
    nz = n // 2
    npz = nz // 2
    me = lax.axis_index("patch")
    tile = lax.axis_index("tile")
    core = tile % 2
    ty = tile // 2
    chunks = acc.shape[0]
    chunk = acc.shape[2]
    zz = me // 2
    xx = me % 2
    h = zz % 2
    mate = me + 2 - 4 * h

    def half_cols(a):
        return pl.ds(pl.multiple_of(a * hw, HEAD), hw)

    loads = []
    for i, (src, dst) in enumerate(
        (
            (wv_hbm, w_vid),
            (wa_hbm, w_aud),
            (wk_hbm.at[:, half_cols(h)], w_qkv.at[:, 0:hw]),
            (wval_hbm.at[:, half_cols(h)], w_qkv.at[:, hw : 2 * hw]),
            (wq_hbm.at[:, half_cols(h)], w_qkv.at[:, 2 * hw : 3 * hw]),
            (wo_hbm, w_o),
            (wf_hbm, w_f),
            (cw_hbm.at[0:width], w_qkv.at[:, 0:out_ch]),
            (cw_hbm.at[width:taps], w_qkv.at[0 : taps - width, out_ch : 2 * out_ch]),
            (wk_hbm.at[:, half_cols(1 - h)], w_qkv.at[:, 3 * hw : 4 * hw]),
            (wval_hbm.at[:, half_cols(1 - h)], w_qkv.at[:, 4 * hw : 5 * hw]),
            (wq_hbm.at[:, half_cols(1 - h)], w_qkv.at[:, 5 * hw : 6 * hw]),
        )
    ):
        loads.append(pltpu.make_async_copy(src, dst, load_sem.at[i]))
    for i in (0, 1, 2, 3, 4, 9, 10, 11, 5, 6):
        loads[i].start()

    got[...] = jnp.zeros(got.shape, BF16)
    barrier = pltpu.get_barrier_semaphore()
    for z, z_there in ((-1, zz > 0), (1, zz < nz - 1)):

        @pl.when(z_there)
        def _():
            pl.semaphore_signal(
                barrier, inc=1, device_id=(me + 2 * z, tile), device_id_type=MESH
            )

    sibling = ty * 2 + 1 - core
    across = (1 - ty) * 2 + core
    for spot in ((me + 1 - 2 * xx, tile), (me, sibling), (me, across)):
        pl.semaphore_signal(barrier, inc=1, device_id=spot, device_id_type=MESH)

    def padded(x):
        return jnp.concatenate([x, jnp.zeros((pad - rows, x.shape[1]), F32)], axis=0)

    line_row = lax.broadcasted_iota(jnp.int32, (pad - rows, HEAD), 0)
    aud_stamps = jnp.concatenate(
        [stamps[:, VID_DEV:rows], jnp.zeros((1, HEAD - AUD_DEV), jnp.int32)], axis=1
    ).astype(F32)
    vid_stamps = stamps[:, 0:VID_DEV].astype(F32)
    tail = jnp.where(line_row == 0, vid_stamps, jnp.where(line_row == 1, aud_stamps, 0.0))
    lat[xx, zz] = jnp.concatenate([latents[...], tail], axis=0).astype(BF16)

    def put_kv(where, slot, i, k, v):
        where[slot, i, 0:VID_DEV] = k[:VID_DEV].astype(BF16)
        where[slot, i, VID_DEV : 2 * VID_DEV] = v[:VID_DEV].astype(BF16)
        last = jnp.concatenate([k[VID_DEV:], v[VID_DEV:]], axis=0)
        where[slot, i, 2 * VID_DEV : 2 * rows] = last.astype(BF16)

    for i in range(nh):
        for a, slot in ((h, 1), (1 - h, n + 2 + zz)):
            cs = pl.ds(pl.multiple_of(a * hw + i * HEAD, HEAD), HEAD)
            put_kv(kv0, slot, i, k_cache[:, cs].astype(F32), v_cache[:, cs].astype(F32))
    pl.semaphore_wait(barrier, 5 - jnp.where((zz == 0) | (zz == nz - 1), 1, 0))

    def remote(src, dst, ss, rs, patch):
        return pltpu.make_async_remote_copy(
            src_ref=src,
            dst_ref=dst,
            send_sem=ss,
            recv_sem=rs,
            device_id=(patch, tile),
            device_id_type=MESH,
        )

    def inside_line(z):
        return (z >= 0) & (z < nz)

    def lat_send(di, d):
        step = 1 - 2 * di
        s = zz - step * (d - 1)
        copy = remote(
            lat.at[xx, s], lat.at[xx, s], lz_ss.at[di, d - 1], lz_rs.at[di, d - 1], me + 2 * step
        )
        return inside_line(s) & inside_line(zz + step), copy

    def lat_arrive(di, d):
        step = 1 - 2 * di
        s = zz - step * d
        copy = remote(
            lat.at[xx, s], lat.at[xx, s], lz_ss.at[di, d - 1], lz_rs.at[di, d - 1], me - 2 * step
        )
        return inside_line(s), s, copy

    def lat_cross(s, line):
        return remote(
            lat.at[line, s], lat.at[line, s], lx_ss.at[s], lx_rs.at[s], me + 1 - 2 * xx
        )

    def lat_event(d):
        for di in range(2):
            there, s, copy = lat_arrive(di, d)

            @pl.when(there)
            def _():
                copy.wait_recv()
                if d + 1 < nz:
                    onward, forward = lat_send(di, d + 1)

                    @pl.when(onward)
                    def _():
                        forward.start()

                lat_cross(s, xx).start()

    def slot_of(z, s, a):
        other = 2 * lax.rem(s // 2 - z // 2 + npz, npz) + s % 2
        slot = jnp.where(s == z, 1, jnp.where(s == z + 1 - 2 * (z % 2), n, other))
        return jnp.where(a == z % 2, slot, n + 2 + s)

    def half_of(di, kind):
        return (1 - di) + kind * (2 * di - 1)

    def wanted_at(di, kind, z):
        return (kind == 0) | (z != (nz - 1 if di == 0 else 0))

    def kv_send(di, d, kind, i):
        step = 1 - 2 * di
        s = zz - step * (d - 1)
        a = half_of(di, kind)
        copy = remote(
            kv0.at[slot_of(zz, s, a), i],
            kv0.at[slot_of(zz + step, s, a), i],
            kz_ss.at[di, d - 1, kind, i],
            kz_rs.at[di, d - 1, kind, i],
            me + 2 * step,
        )
        return inside_line(s) & inside_line(zz + step) & wanted_at(di, kind, zz + step), copy

    def kv_cross(s, i, slot):
        return remote(
            kv0.at[slot, i], kv0.at[nz + s, i], kx_ss.at[s, i], kx_rs.at[s, i], me + 1 - 2 * xx
        )

    def event(e):
        d = e // (2 * nh) + 1
        kind = e // nh % 2
        i = e % nh
        for di in range(2):
            step = 1 - 2 * di
            s = zz - step * d
            a = half_of(di, kind)
            slot = slot_of(zz, s, a)

            @pl.when(inside_line(s) & wanted_at(di, kind, zz))
            def _():
                remote(
                    kv0.at[slot, i],
                    kv0.at[slot, i],
                    kz_ss.at[di, d - 1, kind, i],
                    kz_rs.at[di, d - 1, kind, i],
                    me - 2 * step,
                ).wait_recv()
                onward, forward = kv_send(di, d + 1, kind, i)

                @pl.when(onward)
                def _():
                    forward.start()

                @pl.when(a == h)
                def _():
                    kv_cross(s, i, slot).start()

    def start_own(kind, pieces):
        for i in pieces:
            for di in range(2):
                go, copy = kv_send(di, 1, kind, i)

                @pl.when(go)
                def _():
                    copy.start()

    for di in range(2):
        go, copy = lat_send(di, 1)

        @pl.when(go)
        def _():
            copy.start()

    lat_cross(zz, xx).start()
    start_own(0, (0,))
    kv_cross(zz, 0, 1).start()

    lane = lax.broadcasted_iota(jnp.int32, (1, HEAD), 1)
    frequency = jnp.exp(-jnp.log(F32(10000.0)) * (lane % (HEAD // 2)).astype(F32) / (HEAD // 2))
    times = lax.broadcasted_iota(jnp.int32, (HEAD // 2, HEAD), 0).astype(F32)
    angles = times * frequency
    waves = (jnp.cos(angles), jnp.where(lane < HEAD // 2, -1.0, 1.0) * jnp.sin(angles))
    for k, wave in enumerate(waves):
        top = wave.astype(BF16)
        cs = slice(k * HEAD, (k + 1) * HEAD)
        table[0 : HEAD // 2, cs] = top
        table[HEAD // 2 : HEAD, cs] = (wave - top.astype(F32)).astype(BF16)

    waited = set()

    def need(i):
        if i not in waited:
            loads[i].wait()
            waited.add(i)

    def embed(blocks, step):
        count = len(blocks)
        size = count * rows
        vid_b = jnp.concatenate([b[:VID_DEV] for b in blocks], axis=0).astype(BF16)
        aud_b = jnp.concatenate([b[VID_DEV:rows] for b in blocks], axis=0).astype(BF16)
        square = jnp.zeros((size, 1), F32)
        wide = width // 4
        for i in range(4):
            c = slice(i * wide, (i + 1) * wide)
            e = jnp.concatenate([dot(vid_b, w_vid[:, c]), dot(aud_b, w_aud[:, c])], axis=0)
            emb[0:size, c] = e
            square = square + jnp.sum(e * e, axis=1, keepdims=True)
        scale = lax.rsqrt(square / width + EPSILON)
        for i in range(4):
            c = slice(i * wide, (i + 1) * wide)
            x = emb[0:size, c] * scale * (1.0 + mod_scale[step : step + 1, c])
            normed[0:size, c] = (x + mod_shift[step : step + 1, c]).astype(BF16)

    def shard_rows(x, g, count):
        if count == 1:
            return x
        first = count * VID_DEV + g * AUD_DEV
        return jnp.concatenate(
            [x[g * VID_DEV : (g + 1) * VID_DEV], x[first : first + AUD_DEV]], axis=0
        )

    def rotate(x, gain, cos, sin):
        x = x * lax.rsqrt(jnp.mean(x * x, axis=1, keepdims=True) + EPSILON)
        x = x * gain
        return x * cos + pltpu.roll(x, HEAD // 2, 1) * sin

    def gain_row(gain, a, i):
        return gain[pl.ds((h if a == 0 else 1 - h) * nh + i, 1), :]

    def project_kv(count, a, cos, sin, put):
        raw = dot(normed[0 : count * rows, :], w_qkv[:, 3 * a * hw : (3 * a + 2) * hw])
        for i in range(nh):
            k = rotate(raw[:, i * HEAD : (i + 1) * HEAD], gain_row(k_gain, a, i), cos, sin)
            v = raw[:, hw + i * HEAD : hw + (i + 1) * HEAD]
            for g in range(count):
                put(g, a, i, shard_rows(k, g, count), shard_rows(v, g, count))

    def project_q(count, a, cos, sin, targets):
        raw = dot(normed[0 : count * rows, :], w_qkv[:, (3 * a + 2) * hw : 3 * (a + 1) * hw])
        for i in range(nh):
            gain = gain_row(q_gain, a, i) * SCALE
            q = rotate(raw[:, i * HEAD : (i + 1) * HEAD], gain, cos, sin)
            for g in range(count):
                q_ref[targets[g], i] = padded(shard_rows(q, g, count)).astype(BF16)

    spot = lax.broadcasted_iota(jnp.int32, (HEAD, 3 * HEAD), 0) % (HEAD // 2)

    def pair_waves(blocks):
        aud = jnp.where(
            lane < AUD_DEV,
            blocks[0][rows + 1 : rows + 2],
            pltpu.roll(blocks[1][rows + 1 : rows + 2], AUD_DEV, 1),
        )
        line = jnp.concatenate([b[rows : rows + 1] for b in blocks] + [aud], axis=1)
        chosen = jnp.where(spot == line.astype(jnp.int32), 1.0, 0.0).astype(BF16)
        both = lax.dot_general(
            chosen, table[...], (((0,), (0,)), ((), ())), preferred_element_type=F32
        )
        pair_cs[0] = both[0 : 2 * rows, 0:HEAD]
        pair_cs[1] = both[0 : 2 * rows, HEAD : 2 * HEAD]

    state_ref[...] = padded(latents[...])

    lat_event(1)
    start_own(0, range(1, nh))
    for i in range(1, nh):
        kv_cross(zz, i, 1).start()

    own_blocks = [lat[xx, zz].astype(F32), lat[xx, zz + 1 - 2 * h].astype(F32)]
    need(0)
    need(1)
    embed(own_blocks, 0)

    def keep_near(count):
        for k in range(chunks):
            es = pl.ds(pl.multiple_of(core * wing + k * chunk, HEAD), chunk)
            last = emb[count * VID_DEV : count * VID_DEV + AUD_DEV, es]
            full = padded(jnp.concatenate([emb[0:VID_DEV, es], last], axis=0))
            acc[k] = jnp.where(ty == 0, full[:part_rows], full[part_rows:])

    keep_near(2)
    if nz > 2:
        lat_event(2)
    start_own(1, range(nh))
    pair_waves(own_blocks)
    for k in range(2):
        cs_ref[k] = shard_rows(pair_cs[k], 0, 2)

    def put_own(g, a, i, k, v):
        if a == 0:
            put_kv(kv0, n + 1 if g == 0 else 0, i, k, v)
        if g == 1:
            put_kv(kv1.at[a], 0, i, k, v)

    need(2)
    need(3)
    project_kv(2, 0, pair_cs[0], pair_cs[1], put_own)
    for d in range(3, nz):
        lat_event(d)
    need(4)
    project_q(2, 0, pair_cs[0], pair_cs[1], (0, 1))
    for e in range(nh):
        event(e)
    need(9)
    need(10)
    last_rows = normed[2 * VID_DEV : 2 * rows].astype(F32)[AUD_DEV:]
    normed[0:VID_DEV] = normed[VID_DEV : 2 * VID_DEV]
    normed[VID_DEV:rows] = last_rows.astype(BF16)
    mate_waves = [shard_rows(pair_cs[k], 1, 2) for k in range(2)]

    def put_mate(g, a, i, k, v):
        put_kv(kv1.at[a], 0, i, k, v)

    project_kv(1, 1, mate_waves[0], mate_waves[1], put_mate)
    for e in range(nh, 2 * nh):
        event(e)

    bw = VID_DEV // (nt * FRAMES * BH)
    gw = bw + 2
    slots = 2 * FRAMES
    high, wide_w = n * BH, nt * bw
    share = VID_DEV // (n * nt)
    sent = sel.shape[1]
    room = got.shape[1]
    group = HEAD // room
    row = lax.broadcasted_iota(jnp.int32, (place.shape[0], 1), 0)
    f_id = row % slots - 1
    h_id = row // (slots * gw) - 1 + me * BH
    w_id = row // slots % gw - 1 + tile * bw
    inside = (
        (f_id >= 0)
        & (f_id < FRAMES)
        & (h_id >= 0)
        & (h_id < high)
        & (w_id >= 0)
        & (w_id < wide_w)
    )
    wanted = jnp.where(inside, (f_id * high + h_id) * wide_w + w_id, -1)
    down = lax.broadcasted_iota(jnp.int32, (VID_DEV, VID_DEV), 0)
    along = lax.broadcasted_iota(jnp.int32, (VID_DEV, VID_DEV), 1)

    def block_ranks(cell):
        bh = cell // wide_w % high // BH
        bc = cell % wide_w // bw
        block = (bh * nt + bc).astype(F32)
        column = jnp.sum(jnp.where(down == along, block, 0.0), axis=1, keepdims=True)
        ahead = jnp.where((column == block) & (down < along), 1.0, 0.0)
        return bh, bc, jnp.sum(ahead, axis=0, keepdims=True).astype(jnp.int32)

    def slot_in(ranks, p):
        bh, bc, rank = ranks
        dh = bh - p + 1
        dw = bc - tile + 1
        near_by = (dh >= 0) & (dh < 3) & (dw >= 0) & (dw < 3)
        return jnp.where(near_by, (dh * 3 + dw) * share + rank, -HEAD)

    my_ranks = block_ranks(cells[:, pl.ds(pl.multiple_of(me * VID_DEV, VID_DEV), VID_DEV)])
    pick = lax.broadcasted_iota(jnp.int32, (sent, VID_DEV), 0)
    for j in range(n):
        slot = slot_in(my_ranks, lax.rem(me + j, n))
        sel[j] = jnp.where(pick == slot, 1.0, 0.0).astype(BF16)
    for q in range(n // group):
        found, moved = [], []
        for k in range(group):
            c = slice((q * group + k) * VID_DEV, (q * group + k + 1) * VID_DEV)
            found.append(jnp.where(cells[:, c] == wanted, 1.0, 0.0).astype(BF16))
            slot = slot_in(block_ranks(cells[:, c]), me) + k * room
            moved.append(jnp.where(down == slot, 1.0, 0.0).astype(BF16))
        place[:, q * HEAD : (q + 1) * HEAD] = lax.dot_general(
            jnp.concatenate(found, axis=1),
            jnp.concatenate(moved, axis=1),
            (((1,), (1,)), ((), ())),
            preferred_element_type=F32,
        ).astype(BF16)

    pairs = n // 2
    total_events = (nz - 1) * 2 * nh
    each = -(-(total_events - 2 * nh) // (pairs - 1))
    marks = [each * k // 3 for k in range(4)]

    early = pairs // 4

    def pair_of(j):
        line = j % 2
        turn = j // 2
        first = 2 * lax.rem(zz // 2 + turn, npz)
        side = jnp.where(line == 0, xx, 1 - xx)
        return line, first, side, jnp.where(line == 1, nz + first, 2 * turn)

    def put_at(slot):
        def put(g, a, i, k, v):
            put_kv(kv1.at[a], slot + g, i, k, v)

        return put

    @pl.loop(1, pairs)
    def _(j):
        line, first, side, slot = pair_of(j)

        @pl.when(line == 1)
        def _():
            for g in range(2):
                lat_cross(first + g, 1 - xx).wait_recv()

        blocks = [lat[side, first + g].astype(F32) for g in range(2)]
        embed(blocks, 0)
        base = 2 * nh + (j - 1) * each
        for e in range(marks[0], marks[1]):
            event(base + e)
        pair_waves(blocks)
        project_kv(2, 0, pair_cs[0], pair_cs[1], put_at(slot))
        for e in range(marks[1], marks[2]):
            event(base + e)

        @pl.when(j <= early)
        def _():
            project_kv(2, 1, pair_cs[0], pair_cs[1], put_at(slot))

        for e in range(marks[2], marks[3]):
            event(base + e)

    def late_pairs():
        @pl.loop(early + 1, pairs)
        def _(j):
            line, first, side, slot = pair_of(j)
            blocks = [lat[side, first + g].astype(F32) for g in range(2)]
            embed(blocks, 0)
            pair_waves(blocks)
            project_kv(2, 1, pair_cs[0], pair_cs[1], put_at(slot))

    for j in range(1, n):
        pl.semaphore_signal(
            barrier, inc=1, device_id=(lax.rem(me + j, n), tile), device_id_type=MESH
        )

    def score(keys_of, r, first, i):
        span = slice(first, first + n)
        last = keys_of[span, i, 2 * VID_DEV : 2 * rows].astype(F32)
        last_keys = last[:, :AUD_DEV].reshape(n * AUD_DEV, HEAD).astype(BF16)
        last_values = last[:, AUD_DEV:].reshape(n * AUD_DEV, HEAD).astype(BF16)
        keys = jnp.concatenate(
            [keys_of[span, i, 0:VID_DEV].reshape(n * VID_DEV, HEAD), last_keys], axis=0
        )
        values = jnp.concatenate(
            [keys_of[span, i, VID_DEV : 2 * VID_DEV].reshape(n * VID_DEV, HEAD), last_values],
            axis=0,
        )
        scores = lax.dot_general(
            q_ref[r, i], keys, (((1,), (1,)), ((), ())), preferred_element_type=F32
        )
        return scores, jnp.max(scores, axis=1, keepdims=True), values

    def attend(held):
        scores, top, values = held
        weights = jnp.exp2(scores - top)
        total = jnp.sum(weights, axis=1, keepdims=True)
        return (dot(weights.astype(BF16), values) / total).astype(BF16)

    batch = nh if n * rows <= 2048 else 1

    def attend_all(keys_of, r, first, result):
        for k in range(0, nh, batch):
            held = [score(keys_of, r, first, i) for i in range(k, min(k + batch, nh))]
            for i, parts in enumerate(held):
                result[k + i] = attend(parts)

    for step in range(STEPS):
        state = state_ref[...]
        if step == 0:
            swaps = []
            for i in range(nh):
                for s in range(nz):
                    kv_cross(s, i, nz + s).wait_recv()
                o_send[i] = attend(score(kv0, 1, 0, i))
                copy = remote(o_send.at[i], att.at[h, i], o_ss.at[i], o_rs.at[i], mate)
                copy.start()
                swaps.append(copy)
            attend_all(kv0, 0, 2, att.at[h])
            need(5)
            for i in range(nh):
                remote(
                    o_send.at[i], att.at[1 - h, i], o_ss.at[i], o_rs.at[i], mate
                ).wait_recv()
        else:

            def put_fresh(g, a, i, k, v):
                put_kv(kv1.at[a], 1, i, k, v)

            embed([state], step)
            keep_near(1)
            need(11)
            for a in range(2):
                project_kv(1, a, cs_ref[0], cs_ref[1], put_fresh)
                project_q(1, a, cs_ref[0], cs_ref[1], (a,))
            for i in (7, 8):
                loads[i].start()
            for a in range(2):
                attend_all(kv1.at[a], a, 0, att.at[h if a == 0 else 1 - h])

        heads = [att[a, i] for a in range(2) for i in range(nh)]
        whole = jnp.concatenate(heads, axis=1).astype(F32)
        turned = jnp.concatenate([whole[part_rows:], whole[:part_rows]], axis=0)
        mine_att = jnp.where(ty == 0, turned, whole).astype(BF16)

        def out_part(side, k):
            cs = pl.ds(pl.multiple_of(side * wing + k * chunk, HEAD), chunk)
            return dot(mine_att, w_o[:, cs])

        def tile_copy(src, dst, ss, rs, target):
            return pltpu.make_async_remote_copy(
                src_ref=src,
                dst_ref=dst,
                send_sem=ss,
                recv_sem=rs,
                device_id=(me, target),
                device_id_type=MESH,
            )

        near_rows = pl.ds(pl.multiple_of(ty * part_rows, 8), part_rows)
        first = []
        for k in range(chunks):
            s1_send[k] = out_part(1 - core, k).astype(BF16)
            copy = tile_copy(
                s1_send.at[k], s1_recv.at[k], s1_ss.at[step, k], s1_rs.at[step, k], sibling
            )
            copy.start()
            first.append(copy)
        second = []
        far_parts = []
        for k in range(chunks):
            mine = out_part(core, k)
            first[k].wait_recv()
            mine = mine + s1_recv[k].astype(F32)
            far_parts.append(mine[:part_rows])
            acc[k] += mine[part_rows:]
            if k % 2 == 1:
                j = k // 2
                s2_send[j] = jnp.concatenate(far_parts, axis=0).astype(BF16)
                far_parts = []
                far = tile_copy(
                    s2_send.at[j], s2_recv.at[j], s2_ss.at[step, j], s2_rs.at[step, j], across
                )
                far.start()
                second.append(far)
        if step == 0:
            late_pairs()
        need(6)
        square = jnp.zeros((part_rows, 1), F32)
        part = jnp.zeros((part_rows, w_f.shape[1]), F32)
        for j, far in enumerate(second):
            far.wait_recv()
            came = s2_recv[j].astype(F32)
            for half in range(2):
                k = 2 * j + half
                mixed = acc[k] + came[half * part_rows : (half + 1) * part_rows]
                square = square + jnp.sum(mixed * mixed, axis=1, keepdims=True)
                fs = pl.ds(pl.multiple_of(core * wing + k * chunk, HEAD), chunk)
                part = part + dot((mixed * out_gain[:, fs]).astype(BF16), w_f[fs, :])
        channels = part.shape[1]
        vel_send[...] = jnp.concatenate(
            [part, jnp.broadcast_to(square, (part_rows, HEAD))], axis=1
        )
        near = tile_copy(vel_send, vel_recv, v_ss.at[step, 0], v_rs.at[step, 0], sibling)
        near.start()
        near.wait_recv()
        both = vel_send[...] + vel_recv[...]
        scale = lax.rsqrt(both[:, channels : channels + 1] / width + EPSILON)
        fresh = state_ref[near_rows, :] - step_sizes[step] * (both[:, :channels] * scale)
        st_send[...] = fresh
        over = tile_copy(st_send, st_recv.at[step], v_ss.at[step, 1], v_rs.at[step, 1], across)
        over.start()
        over.wait_recv()
        other = st_recv[step]
        new_state = jnp.concatenate(
            [jnp.where(ty == 0, fresh, other), jnp.where(ty == 0, other, fresh)], axis=0
        )
        state_ref[...] = new_state
        for copy in first + second + [near, over] + (swaps if step == 0 else []):
            copy.wait_send()

    mine = dot(sel[...].reshape(n * sent, VID_DEV), state_ref[0:VID_DEV, :].astype(BF16))
    vid[...] = mine.astype(BF16).reshape(n, sent, HEAD)
    sends = []
    pl.semaphore_wait(barrier, n - 1)
    for j in range(1, n):
        copy = remote(
            vid.at[j], got.at[me, 0:sent], vid_ss.at[j], vid_rs.at[j], lax.rem(me + j, n)
        )
        copy.start()
        sends.append(copy)
    got[me, 0:sent] = vid[0]
    state_out[...] = state_ref[0:rows, :]

    for di in range(2):
        for d in range(1, nz):
            go, copy = lat_send(di, d)

            @pl.when(go)
            def _():
                copy.wait_send()

    for s in range(nz):
        lat_cross(s, xx).wait_send()
        for i in range(nh):
            kv_cross(s, i, 1).wait_send()

    @pl.loop(0, total_events)
    def _(e):
        for di in range(2):
            go, copy = kv_send(di, e // (2 * nh) + 1, e // nh % 2, e % nh)

            @pl.when(go)
            def _():
                copy.wait_send()

    need(7)
    need(8)
    for j in range(1, n):
        source = lax.rem(me - j + n, n)
        landed = got.at[source, 0:sent]
        remote(vid.at[j], landed, vid_ss.at[j], vid_rs.at[j], source).wait_recv()
    grown[...] = dot(place[...], got[...].reshape(n * room, HEAD))
    pieces = []
    for a in range(3):
        for b in range(3):
            for c in range(3):
                starts = [
                    ((h_off + b) * gw + w + c) * slots + a
                    for h_off in range(BH)
                    for w in range(bw)
                ]
                pieces.append(
                    jnp.concatenate([grown[s : s + FRAMES, :] for s in starts], axis=0).astype(BF16)
                )
    cut = width // HEAD
    total = dot(jnp.concatenate(pieces[:cut], axis=1), w_qkv[:, 0:out_ch])
    rest = w_qkv[0 : taps - width, out_ch : 2 * out_ch]
    total = total + dot(jnp.concatenate(pieces[cut:], axis=1), rest)
    conv_out[...] = total + conv_b[...]
    for copy in sends:
        copy.wait_send()


def finish(state, conv, state_out, decoded):
    state_out[...] = state[...]
    bw = decoded.shape[2]
    for h in range(BH):
        for w in range(bw):
            first = (h * bw + w) * FRAMES
            decoded[:, h, w, :] = conv[first : first + FRAMES, :].astype(BF16)


def local(
    latents,
    timestamps,
    cell_map,
    w_video,
    w_audio,
    mod_scale,
    mod_shift,
    w_query,
    w_key,
    w_value,
    q_gain,
    k_gain,
    k_cache,
    v_cache,
    w_out,
    out_gain,
    w_final,
    step_sizes,
    conv_w,
    conv_b,
):
    n, nt = lax.axis_size("patch"), lax.axis_size("tile")
    rows, channels = latents.shape
    width = w_query.shape[0]
    cols = w_query.shape[1]
    pad = -(-rows // 16) * 16
    part_rows = pad // (nt // 2)
    wing = width // 2
    chunk = 256
    chunks = wing // chunk
    nz = n // 2
    hw = cols // 2
    nh = hw // HEAD
    bw = VID_DEV // (nt * FRAMES * BH)
    border = (BH + 2) * (bw + 2) * 2 * FRAMES
    cells = FRAMES * BH * bw
    sent = -(-9 * VID_DEV // (n * nt * 16)) * 16
    room = next(r for r in (16, 32, 64, 128) if r >= sent)
    out_ch = conv_w.shape[-1]
    conv_flat = conv_w.reshape(-1, out_ch)
    vmem = pl.BlockSpec(memory_space=pltpu.VMEM)
    hbm = pl.BlockSpec(memory_space=pl.ANY)
    dma = pltpu.SemaphoreType.DMA
    state, conv = pl.pallas_call(
        functools.partial(kernel, n, nt),
        out_shape=(
            jax.ShapeDtypeStruct((rows, channels), F32),
            jax.ShapeDtypeStruct((cells, out_ch), F32),
        ),
        in_specs=[vmem] * 10 + [pl.BlockSpec(memory_space=pltpu.SMEM), vmem] + [hbm] * 8,
        out_specs=(vmem, vmem),
        scratch_shapes=[
            pltpu.VMEM(w_video.shape, BF16),
            pltpu.VMEM(w_audio.shape, BF16),
            pltpu.VMEM((width, 6 * hw), BF16),
            pltpu.VMEM(w_out.shape, BF16),
            pltpu.VMEM(w_final.shape, BF16),
            pltpu.VMEM((n + 2 + nz, nh, 2 * rows, HEAD), BF16),
            pltpu.VMEM((2, n, nh, 2 * rows, HEAD), BF16),
            pltpu.VMEM((2, nz, pad, HEAD), BF16),
            pltpu.VMEM((2 * rows, width), F32),
            pltpu.VMEM((2 * rows, width), BF16),
            pltpu.VMEM((2, nh, pad, HEAD), BF16),
            pltpu.VMEM((2, rows, HEAD), F32),
            pltpu.VMEM((2, 2 * rows, HEAD), F32),
            pltpu.VMEM((HEAD, 2 * HEAD), BF16),
            pltpu.VMEM((2, nh, pad, HEAD), BF16),
            pltpu.VMEM((nh, pad, HEAD), BF16),
            pltpu.VMEM((pad, channels), F32),
            pltpu.VMEM((part_rows, channels), F32),
            pltpu.VMEM((STEPS, part_rows, channels), F32),
            pltpu.VMEM((chunks, part_rows, chunk), F32),
            pltpu.VMEM((chunks, pad, chunk), BF16),
            pltpu.VMEM((chunks, pad, chunk), BF16),
            pltpu.VMEM((chunks // 2, pad, chunk), BF16),
            pltpu.VMEM((chunks // 2, pad, chunk), BF16),
            pltpu.VMEM((part_rows, channels + HEAD), F32),
            pltpu.VMEM((part_rows, channels + HEAD), F32),
            pltpu.VMEM((n, sent, channels), BF16),
            pltpu.VMEM((n, room, channels), BF16),
            pltpu.VMEM((n, sent, VID_DEV), BF16),
            pltpu.VMEM((border, n * room), BF16),
            pltpu.VMEM((border, channels), F32),
            dma((12,)),
            dma((2, nz - 1)),
            dma((2, nz - 1)),
            dma((nz,)),
            dma((nz,)),
            dma((2, nz - 1, 2, nh)),
            dma((2, nz - 1, 2, nh)),
            dma((nz, nh)),
            dma((nz, nh)),
            dma((nh,)),
            dma((nh,)),
            dma((STEPS, chunks)),
            dma((STEPS, chunks)),
            dma((STEPS, chunks // 2)),
            dma((STEPS, chunks // 2)),
            dma((STEPS, 2)),
            dma((STEPS, 2)),
            dma((n,)),
            dma((n,)),
        ],
        compiler_params=pltpu.CompilerParams(
            collective_id=0, has_side_effects=True, vmem_limit_bytes=63 * 1024 * 1024
        ),
    )(
        latents,
        timestamps.reshape(1, -1),
        cell_map.reshape(1, -1),
        mod_scale,
        mod_shift,
        q_gain.reshape(-1, HEAD),
        k_gain.reshape(-1, HEAD),
        k_cache,
        v_cache,
        out_gain.reshape(1, -1),
        step_sizes,
        conv_b.reshape(1, -1),
        w_video,
        w_audio,
        w_query,
        w_key,
        w_value,
        w_out,
        w_final,
        conv_flat,
    )
    return pl.pallas_call(
        finish,
        out_shape=(
            jax.ShapeDtypeStruct((rows, channels), F32),
            jax.ShapeDtypeStruct((FRAMES, BH, bw, out_ch), BF16),
        ),
        in_specs=[vmem, vmem],
        out_specs=(vmem, vmem),
    )(state, conv)


def solution(mesh):
    return jax.shard_map(
        local,
        mesh=mesh,
        in_specs=(
            P("patch", None),
            P("patch"),
            P(),
            P(),
            P(),
            P(),
            P(),
            P(None, "tile"),
            P(None, "tile"),
            P(None, "tile"),
            P("tile"),
            P("tile"),
            P("patch", "tile"),
            P("patch", "tile"),
            P("tile", None),
            P(),
            P(),
            P(),
            P(),
            P(),
        ),
        out_specs=(P("patch", None), P(None, "patch", "tile", None)),
        check_vma=False,
    )
```
